256 devices in a mesh: rep: 8 (over y, z_hi), ep: 32 (over x, z_lo, core).
Axes of the slice: x: 4, y: 4, z: 8 (z_hi: 2, z_lo: 4; z = z_hi * 4 + z_lo), core: 2. Of those that a mesh axis runs over, the one named last changes fastest.
Arguments:
- out_grad: bfloat16 [65536, 3584], P(('rep', 'ep')), may hold values from -0.8984375 to 0.8984375
- expert_ids: int32 [65536, 8], P(('rep', 'ep')), may hold values from 0 to 255, as said below
- slots: int32 [65536, 8], P(('rep', 'ep')), may hold values from -1 to 11, as said below
- gate_weights: bfloat16 [65536, 8], P(('rep', 'ep')), may hold values from 0.049804688 to 0.59765625
- saved_gate_up: bfloat16 [8, 32, 384, 2048], P('rep', 'ep'), may hold values from -6 to 6
- master: float32 [32, 1024, 3584], P('ep', 'rep'), may hold values from -0.1875 to 0.1875
- moment1: bfloat16 [32, 1024, 3584], P('ep', 'rep'), may hold values from -0.59765625 to 0.59765625
- moment2: bfloat16 [32, 1024, 3584], P('ep', 'rep'), may hold values from 0.0009994507 to 0.0099487305
Outputs:
- grad_gate_up: bfloat16 [8, 32, 384, 2048], P('rep', 'ep')
- gate_grad: float32 [65536, 8], P(('rep', 'ep'))
- master_out: float32 [32, 1024, 3584], P('ep', 'rep')
- moment1_out: bfloat16 [32, 1024, 3584], P('ep', 'rep')
- moment2_out: bfloat16 [32, 1024, 3584], P('ep', 'rep')
The draws below stay inside these ranges and needn't reach their ends.
Inputs may be any that keep to these rules, and one draw needn't show every extreme that they name: `expert_ids`: each row names 8 different experts of 0 to 255. Within the rows of one device, the choices naming one expert, taken in order of token then choice, have slots 0, 1, 2 and so on; those from 12 on are -1. Every device has an expert of the window with more than 12 such choices.
All inputs are finite; a program needn't handle non-finite values.
Results may differ from the reference program's by a relative error of at most 0.025.
Values may be sent and summed in bfloat16 or wider, within the bound.
A program may use at most 128 MiB of HBM per device.

```python
import math
import jax
import jax.numpy as jnp
from jax import lax

DW = 3584
FW = 1024
TOPK = 8
EXP_LOCAL = 8
TOK_DEV = 256
SEND = 12
SLOTS = 384
EXPERTS = 32
TOKENS = 65536
N_REP = 8
N_EP = 32


def route_table(key):
    total_rows = TOK_DEV * N_EP * N_REP
    experts_all = EXP_LOCAL * N_EP
    blocks = N_EP * N_REP
    key_noise, key_level, key_hot = jax.random.split(key, 3)
    noise = jax.random.randint(key_noise, (total_rows, experts_all), 0, 65536)
    level = jax.random.randint(key_level, (experts_all,), 0, 4)
    hot = jax.random.randint(key_hot, (blocks,), 0, N_EP) * EXP_LOCAL
    row_block = jnp.arange(total_rows) // TOK_DEV
    row_inner = jnp.arange(total_rows) % TOK_DEV
    columns = jnp.arange(experts_all)
    planted = (row_inner < SEND + 4)[:, None] & (columns[None, :] == hot[row_block][:, None])
    score = (noise + level[None, :] * 1024) * 256 + columns[None, :] + planted.astype(jnp.int32) * (1 << 27)
    chosen = lax.top_k(score, TOPK)[1]
    return chosen.astype(jnp.int32)


def draw_expert_ids(key, part):
    return route_table(key)


def draw_slots(key, part):
    chosen = route_table(key)
    experts_all = EXP_LOCAL * N_EP
    blocks = N_EP * N_REP
    flat = chosen.reshape(blocks, TOK_DEV * TOPK)

    def block_slots(block_ids):
        onehot = (block_ids[:, None] == jnp.arange(experts_all)[None, :]).astype(jnp.int32)
        rank = jnp.cumsum(onehot, axis=0) - 1
        mine = jnp.sum(rank * onehot, axis=1)
        return jnp.where(mine < SEND, mine, -1).astype(jnp.int32)
    result = lax.map(block_slots, flat)
    return result.reshape(TOK_DEV * N_EP * N_REP, TOPK)


def levels(rng, dims, cuts, low, high):
    level, own = 1.0, jax.random.fold_in(rng, 6)
    for dim, shards_of in cuts:
        steps = jnp.exp(jax.random.uniform(jax.random.fold_in(own, dim), (shards_of,), jnp.float32, low / len(cuts), high / len(cuts)))
        level = level * jnp.repeat(steps, dims[dim] // shards_of).reshape([-1 if axis == dim else 1 for axis in range(len(dims))])
    return level


def scatter_about(rng, dims, width, limit, cuts=(), held_as=jnp.bfloat16):
    loudness = levels(rng, dims, cuts, -0.22, 0.18) if cuts else 1.0
    array = jax.random.normal(rng, dims, jnp.float32) * width * loudness
    return jnp.minimum(jnp.maximum(array, -limit), limit).astype(held_as)


def setup_inputs(seed: int = 0) -> dict:
    keys = jax.random.split(jax.random.key(seed), 9)
    out_grad = scatter_about(keys[0], (TOKENS, DW), 0.15, 0.8984375, ((0, 256),))
    expert_ids = draw_expert_ids(jax.random.fold_in(keys[8], 71), 0)
    slots = draw_slots(jax.random.fold_in(keys[8], 71), 0)
    gate_weights = jnp.clip(0.049804688 + 0.54785156 * jax.random.uniform(keys[3], (TOKENS, TOPK), jnp.float32) ** levels(keys[3], (TOKENS, TOPK), ((0, 256),), -0.2, 0.2), 0.049804688, 0.59765625).astype(jnp.bfloat16)
    saved_gate_up = scatter_about(keys[4], (N_REP, EXPERTS, SLOTS, 2 * FW), 1.0, 6.0, ((0, 8), (1, 32)))
    master = scatter_about(keys[5], (EXPERTS, FW, DW), FW ** -0.5, 0.1875, ((0, 32), (1, 8)), jnp.float32)
    moment1 = scatter_about(keys[6], (EXPERTS, FW, DW), 0.1, 0.59765625, ((0, 32), (1, 8)))
    moment2 = jnp.clip(jnp.exp(math.log(0.0099487305) - 2.2979944 * jax.random.uniform(keys[7], (EXPERTS, FW, DW), jnp.float32) ** levels(keys[7], (EXPERTS, FW, DW), ((0, 32), (1, 8)), -0.2, 0.2)), 0.0009994507, 0.0099487305).astype(jnp.bfloat16)
    return {"out_grad": out_grad, "expert_ids": expert_ids, "slots": slots, "gate_weights": gate_weights, "saved_gate_up": saved_gate_up, "master": master, "moment1": moment1, "moment2": moment2}


beta_one = 0.9
beta_two = 0.95
learn_rate = 0.002
decay_rate = 0.1
adam_eps = 1e-08
adam_step = 50

def swiglu_backward(gate_up, weights, grad_proj):
    half_width = gate_up.shape[-1] // 2
    gate_part = gate_up[..., :half_width].astype(jnp.float32)
    up_part = gate_up[..., half_width:].astype(jnp.float32)
    sigmoid_gate = jax.nn.sigmoid(gate_part)
    silu_gate = gate_part * sigmoid_gate
    hidden = lax.optimization_barrier((silu_gate * up_part).astype(jnp.bfloat16))
    scale = weights.astype(jnp.float32)[..., None]
    scaled = (scale * hidden.astype(jnp.float32)).astype(jnp.bfloat16)
    grad_hidden = scale * grad_proj
    d_gate = grad_hidden * up_part * sigmoid_gate * (1.0 + gate_part * (1.0 - sigmoid_gate))
    d_up = grad_hidden * silu_gate
    return (hidden, scaled, jnp.concatenate([d_gate, d_up], axis=-1).astype(jnp.bfloat16))

def adamw(master, moment1, moment2, grad):
    m_new = beta_one * moment1.astype(jnp.float32) + (1.0 - beta_one) * grad
    v_new = beta_two * moment2.astype(jnp.float32) + (1.0 - beta_two) * grad * grad
    corr_one = 1.0 - beta_one ** adam_step
    corr_two = 1.0 - beta_two ** adam_step
    update = m_new / corr_one / (jnp.sqrt(v_new / corr_two) + adam_eps)
    master_new = master - learn_rate * (update + decay_rate * master)
    return (master_new, m_new.astype(jnp.bfloat16), v_new.astype(jnp.bfloat16))

def reference(out_grad, expert_ids, slots, gate_weights, saved_gate_up, master, moment1, moment2):
    rows_rep = N_EP * TOK_DEV
    dump = EXPERTS * SLOTS
    weight_bf = lax.optimization_barrier(master.astype(jnp.bfloat16))
    weight_f = weight_bf.astype(jnp.float32)
    grads = out_grad.reshape(N_REP, rows_rep, DW)
    id_all = expert_ids.reshape(N_REP, rows_rep, TOPK)
    slot_all = slots.reshape(N_REP, rows_rep, TOPK)
    weight_all = gate_weights.reshape(N_REP, rows_rep, TOPK)

    def one_replica(total, pieces):
        grad_rows, id_rows, slot_rows, weight_rows, gate_up = pieces
        live = (id_rows % EXP_LOCAL == 0) & (slot_rows >= 0)
        source = (jnp.arange(rows_rep, dtype=jnp.int32) // TOK_DEV)[:, None]
        position = jnp.where(live, id_rows // EXP_LOCAL * SLOTS + source * SEND + slot_rows, dump).astype(jnp.int32)
        token_of = jnp.broadcast_to(jnp.arange(rows_rep, dtype=jnp.int32)[:, None], position.shape)
        source_row = jnp.full((dump + 1,), rows_rep, jnp.int32).at[position.reshape(-1)].set(token_of.reshape(-1))[:dump]
        padded = jnp.concatenate([grad_rows, jnp.zeros((1, DW), grad_rows.dtype)], axis=0)
        dout = padded[source_row].reshape(EXPERTS, SLOTS, DW)
        slot_weight = jnp.zeros((dump + 1,), weight_rows.dtype).at[position.reshape(-1)].set(weight_rows.reshape(-1))
        slot_weight = slot_weight[:dump].reshape(EXPERTS, SLOTS)
        dout_f = dout.astype(jnp.float32)
        grad_proj = jnp.einsum('esd,efd->esf', dout_f, weight_f, precision=lax.Precision.HIGHEST)
        hidden, scaled, grad_gate_up = swiglu_backward(gate_up, slot_weight, grad_proj)
        partial_value = jnp.einsum('esf,esd->efd', scaled.astype(jnp.float32), dout_f, precision=lax.Precision.HIGHEST)
        partial_value = lax.optimization_barrier(partial_value.astype(jnp.bfloat16)).astype(jnp.float32)
        expert_out = jnp.einsum('esf,efd->esd', hidden.astype(jnp.float32), weight_f, precision=lax.Precision.HIGHEST)
        expert_out = expert_out.astype(jnp.bfloat16).reshape(dump, DW)
        out_pad = jnp.concatenate([expert_out, jnp.zeros((1, DW), jnp.bfloat16)], axis=0)
        grad_f = grad_rows.astype(jnp.float32)
        scores = [lax.optimization_barrier(jnp.sum(grad_f * out_pad[position[:, which]].astype(jnp.float32), axis=-1)) for which in range(TOPK)]
        gate_grad = jnp.where(live, jnp.stack(scores, axis=1), jnp.zeros((), jnp.float32))
        return (total + partial_value, (grad_gate_up, gate_grad))
    start = jnp.zeros((EXPERTS, FW, DW), jnp.float32)
    grad, outputs = lax.scan(one_replica, start, (grads, id_all, slot_all, weight_all, saved_gate_up))
    grad_gate_up, gate_grad = outputs
    master_out, moment1_out, moment2_out = adamw(master, moment1, moment2, grad)
    return (grad_gate_up, gate_grad.reshape(TOKENS, TOPK), master_out, moment1_out, moment2_out)
```

```python
import functools

import jax
import jax.numpy as jnp
from jax import lax
from jax.experimental import pallas as pl
from jax.experimental.pallas import tpu as pltpu
from jax.sharding import PartitionSpec as P

TOPK = 8
EXP_LOCAL = 8
SEND = 12
PARTS = 4
CHUNKS = (3, 4)
TILE = 512
MESH = pl.DeviceIdType.MESH

beta_one = 0.9
beta_two = 0.95
learn_rate = 0.002
decay_rate = 0.1
adam_eps = 1e-08
adam_step = 50


def adamw(master, moment1, moment2, grad):
    m_new = beta_one * moment1.astype(jnp.float32) + (1.0 - beta_one) * grad
    v_new = beta_two * moment2.astype(jnp.float32) + (1.0 - beta_two) * grad * grad
    corr_one = 1.0 - beta_one**adam_step
    corr_two = 1.0 - beta_two**adam_step
    update = m_new / corr_one / (jnp.sqrt(v_new / corr_two) + adam_eps)
    master_new = master - learn_rate * (update + decay_rate * master)
    return (master_new, m_new.astype(jnp.bfloat16), v_new.astype(jnp.bfloat16))


def iota(shape, dim):
    return lax.broadcasted_iota(jnp.int32, shape, dim)


def div(x, by, top):
    shift = 20
    factor = (1 << shift) // by + 1
    assert all((v * factor) >> shift == v // by for v in range(top)) and top * factor < 2**31
    return (x * factor) >> shift


def kernel(
    n_ep, n_rep,
    ids_ref, slots_ref, gates_ref, og_hbm, gu_hbm, master_hbm,
    ggu_out, gate_out, grad_out,
    og, gu, master, pick, unpick,
    rows_out, rows_in, w_out, w_in, dout, wcol,
    hidden, d_silu, silu, scaled_t, shards,
    s1, r1, keep, s2own, r2own, s2sum, r2sum, own, zs, zr,
    gg_acc, gg_out, gg_in,
    load_sem, rows_ssem, rows_rsem, small_ssem, small_rsem, local_sem, ssem, rsem,
):
    f32, bf16 = jnp.float32, jnp.bfloat16
    r, e = lax.axis_index("rep"), lax.axis_index("ep")
    y, h = lax.div(r, 2), lax.rem(r, 2)
    n_y = n_rep // 2
    up = (lax.rem(r + 2, n_rep), e)
    down = (lax.rem(r + n_rep - 2, n_rep), e)
    across = (r + 1 - 2 * h, e)
    width = og.shape[1]
    part_rows = shards.shape[0] // n_rep
    pair = 2 * part_rows
    msg = PARTS * SEND
    offsets = [sum(CHUNKS[:i]) * PARTS * 128 for i in range(len(CHUNKS))]

    def peer(k):
        return lax.rem(e + k, n_ep)

    loads = [
        pltpu.make_async_copy(src, dst, load_sem.at[i])
        for i, (src, dst) in enumerate(((og_hbm, og), (master_hbm, master), (gu_hbm, gu)))
    ]
    for load in loads:
        load.start()

    barrier = pltpu.get_barrier_semaphore()

    def greet(k, _):
        pl.semaphore_signal(barrier, inc=1, device_id=(r, peer(k)), device_id_type=MESH)
        return _

    lax.fori_loop(1, n_ep, greet, 0)
    for other in (up, down, across):
        pl.semaphore_signal(barrier, inc=1, device_id=other, device_id_type=MESH)

    ids, slots = ids_ref[...], slots_ref[...]
    live = ((ids & (EXP_LOCAL - 1)) == 0) & (slots >= 0)
    expert = ids >> 3
    pos12 = jnp.where(live, expert * SEND + slots, -64)
    pos16 = jnp.where(live, expert * 16 + slots, -64)
    gates = gates_ref[...]
    n_tok = ids.shape[1]

    def weight_rows(b, _):
        row = iota((64, n_tok), 0) + b * 64
        total = jnp.zeros((64, n_tok), f32)
        for k in range(TOPK):
            total += jnp.where(row == pos16[k : k + 1, :], gates[k : k + 1, :], 0.0)
        column = jnp.sum(total, axis=1, keepdims=True)
        w_out[pl.ds(pl.multiple_of(b * 64, 64), 64), :] = jnp.broadcast_to(column, (64, 128)).astype(bf16)
        return _

    lax.fori_loop(0, n_ep * 16 // 64, weight_rows, 0)

    def pick_rows(g, _):
        row = iota((PARTS * msg, n_tok), 0)
        dest = div(row, msg, PARTS * msg)
        rest = row - dest * msg
        part = div(rest, SEND, msg)
        target = (dest + g * PARTS) * SEND + rest - part * SEND
        hit = target == pos12[0:1, :]
        for k in range(1, TOPK):
            hit = hit | (target == pos12[k : k + 1, :])
        for q in range(PARTS):
            one = jnp.where(hit & (part == q), 1.0, 0.0).astype(bf16)
            pick[pl.ds(pl.multiple_of(g * PARTS * msg, 16), PARTS * msg), q * n_tok : (q + 1) * n_tok] = one
        return _

    lax.fori_loop(0, n_ep // PARTS, pick_rows, 0)

    mine = pl.ds(pl.multiple_of(r * part_rows, part_rows), part_rows)
    loads[1].wait()

    def cast(t, _):
        cols = pl.ds(pl.multiple_of(t * TILE, TILE), TILE)
        shards[mine, cols] = master[:, cols].astype(bf16)
        return _

    lax.fori_loop(0, width // TILE, cast, 0)

    def remote(src, dst, i, other):
        return pltpu.make_async_remote_copy(
            src_ref=src, dst_ref=dst, send_sem=ssem.at[i], recv_sem=rsem.at[i],
            device_id=other, device_id_type=MESH,
        )

    pl.semaphore_wait(barrier, n_ep - 1 + 3)

    def shard(rep):
        return shards.at[pl.ds(pl.multiple_of(rep * part_rows, part_rows), part_rows)]

    def half_shard(rep, which):
        half = part_rows // 2
        return shards.at[pl.ds(pl.multiple_of(rep * part_rows + which * half, half), half)]

    started = []

    def start(copy):
        copy.start()
        started.append(copy)
        return copy

    ag_up = start(remote(shard(r), shard(r), 0, up))
    ag_down = start(remote(shard(r), shard(r), 1, down))

    def small(src_of, dst, rows, sems):
        def send(k, _):
            to = peer(k)
            pltpu.make_async_remote_copy(
                src_ref=src_of(to), dst_ref=dst.at[pl.ds(pl.multiple_of(e * rows, rows), rows)],
                send_sem=small_ssem.at[sems], recv_sem=small_rsem.at[sems],
                device_id=(r, to), device_id_type=MESH,
            ).start()
            return _

        lax.fori_loop(1, n_ep, send, 0)
        copy = pltpu.make_async_copy(
            src_of(e), dst.at[pl.ds(pl.multiple_of(e * rows, rows), rows)], local_sem.at[sems]
        )
        copy.start()
        return copy

    def all_of(ref, rows, sem):
        part = ref.at[pl.ds(0, (n_ep - 1) * rows)]
        return pltpu.make_async_copy(part, part, sem)

    w_local = small(lambda to: w_out.at[pl.ds(pl.multiple_of(to * 16, 16), 16)], w_in, 16, 0)

    loads[0].wait()
    rows_local = []
    for p, size in enumerate(CHUNKS):
        wide = size * 128
        out, into = rows_out[p], rows_in[p]

        def gather(g, _, out=out, wide=wide, p=p):
            where = pl.ds(pl.multiple_of(g * PARTS * msg, 16), PARTS * msg)
            total = jnp.zeros((PARTS * msg, wide), f32)
            for q in range(PARTS):
                total += jnp.dot(
                    pick[where, q * n_tok : (q + 1) * n_tok],
                    og[:, offsets[p] + q * wide : offsets[p] + (q + 1) * wide],
                    preferred_element_type=f32,
                )
            out[where, :] = total.astype(bf16)
            return _

        lax.fori_loop(0, n_ep // PARTS, gather, 0)

        def block(ref, i):
            return ref.at[pl.ds(pl.multiple_of(i * msg, 16), msg)]

        def send(k, _, out=out, into=into, p=p):
            to = peer(k)
            pltpu.make_async_remote_copy(
                src_ref=block(out, to), dst_ref=block(into, e),
                send_sem=rows_ssem.at[p], recv_sem=rows_rsem.at[p],
                device_id=(r, to), device_id_type=MESH,
            ).start()
            return _

        lax.fori_loop(1, n_ep, send, 0)
        copy = pltpu.make_async_copy(block(out, e), block(into, e), local_sem.at[2 + p])
        copy.start()
        rows_local.append(copy)

    loads[2].wait()
    n_hidden = hidden.shape[1]
    step = 128

    def activation(t, _):
        cols = pl.ds(pl.multiple_of(t * step, step), step)
        up_cols = pl.ds(pl.multiple_of(n_hidden + t * step, step), step)
        gate, lift = gu[:, cols].astype(f32), gu[:, up_cols].astype(f32)
        sig = jax.nn.sigmoid(gate)
        act = gate * sig
        hidden[:, cols] = (act * lift).astype(bf16)
        silu[:, cols] = act
        d_silu[:, cols] = lift * sig * (1.0 + gate * (1.0 - sig))
        return _

    lax.fori_loop(0, n_hidden // step, activation, 0)
    side = PARTS * msg
    row = iota((side, side), 0)
    part = div(row, msg, side)
    rest = row - part * msg
    dest = div(rest, SEND, msg)
    unpick[...] = jnp.where(
        iota((side, side), 1) == dest * msg + part * SEND + rest - dest * SEND, 1.0, 0.0
    ).astype(bf16)

    w_local.wait()
    all_of(w_in, 16, small_rsem.at[0]).wait()
    n_slots = n_ep * SEND
    row = iota((n_slots, n_ep * 16), 0)
    dest = div(row, SEND, n_slots)
    order = jnp.where(iota(row.shape, 1) == row + dest * (16 - SEND), 1.0, 0.0).astype(bf16)
    wcol[...] = jnp.dot(order, w_in[...], preferred_element_type=f32)

    def scale(t, _):
        cols = pl.ds(pl.multiple_of(t * step, step), step)
        value = wcol[...] * hidden[:, cols].astype(f32)
        scaled_t[cols, :] = value.astype(bf16).astype(f32).T.astype(bf16)
        return _

    lax.fori_loop(0, n_hidden // step, scale, 0)

    ag_up.wait_recv()
    ag_up2 = start(remote(half_shard(down[0], 0), half_shard(down[0], 0), 2, up))
    ag_down.wait_recv()
    ag_down2 = start(remote(half_shard(up[0], 1), half_shard(up[0], 1), 3, down))

    def span(p):
        return pl.ds(offsets[p], CHUNKS[p] * PARTS * 128)

    def tiles(p, body):
        def one(t, _):
            body(pl.ds(pl.multiple_of(offsets[p] + t * TILE, TILE), TILE))
            return _

        lax.fori_loop(0, CHUNKS[p] * PARTS * 128 // TILE, one, 0)

    def arrive(p):
        wide = CHUNKS[p] * 128
        rows_local[p].wait()
        all_of(rows_in[p], msg, rows_rsem.at[p]).wait()

        def restore(g, _):
            got = jnp.dot(
                unpick[...],
                rows_in[p][pl.ds(pl.multiple_of(g * side, 16), side), :],
                preferred_element_type=f32,
            ).astype(bf16)
            for q in range(PARTS):
                dout[pl.ds(pl.multiple_of(g * msg, 16), msg), offsets[p] + q * wide : offsets[p] + (q + 1) * wide] = (
                    got[q * msg : (q + 1) * msg]
                )
            return _

        lax.fori_loop(0, n_ep // PARTS, restore, 0)

    def product(to_y, cols):
        rows = pl.ds(pl.multiple_of(to_y * pair, pair), pair)
        return jnp.dot(scaled_t[rows, :], dout[:, cols], preferred_element_type=f32)

    y_up, y_down, y_far = lax.rem(y + 1, n_y), lax.rem(y + n_y - 1, n_y), lax.rem(y + 2, n_y)
    first, second = pl.ds(0, part_rows), pl.ds(part_rows, part_rows)
    base = 9
    flights = {}

    def stage_one(p):
        def far(cols):
            s1[:, cols] = product(y_far, cols).astype(bf16)

        tiles(p, far)
        i = base + 7 * p
        flights[p, "a"] = start(remote(s1.at[first, span(p)], r1.at[first, span(p)], i, up))
        flights[p, "b"] = start(remote(s1.at[second, span(p)], r1.at[second, span(p)], i + 1, down))

        def near(cols):
            got = product(y_up, cols)
            keep[first, cols] = got[:part_rows]
            s2own[second, cols] = got[part_rows:].astype(bf16)
            got = product(y_down, cols)
            s2own[first, cols] = got[:part_rows].astype(bf16)
            keep[second, cols] = got[part_rows:]

        tiles(p, near)
        flights[p, "own_b"] = start(remote(s2own.at[second, span(p)], r2own.at[second, span(p)], i + 2, up))
        flights[p, "own_a"] = start(remote(s2own.at[first, span(p)], r2own.at[first, span(p)], i + 3, down))

        def here(cols):
            own[:, cols] = product(y, cols)

        tiles(p, here)

    def stage_two(p):
        i = base + 7 * p
        for name, rows, other, j in (("a", first, up, i + 4), ("b", second, down, i + 5)):
            flights[p, name].wait_recv()

            def add(cols, rows=rows):
                s2sum[rows, cols] = (keep[rows, cols] + r1[rows, cols].astype(f32)).astype(bf16)

            tiles(p, add)
            flights[p, "sum_" + name] = start(remote(s2sum.at[rows, span(p)], r2sum.at[rows, span(p)], j, other))

    def stage_three(p):
        for name in ("own_a", "own_b", "sum_a", "sum_b"):
            flights[p, name].wait_recv()

        def half(which, cols):
            rows = pl.ds(pl.multiple_of(which * part_rows, part_rows), part_rows)
            return own[rows, cols] + (r2own[rows, cols].astype(f32) + r2sum[rows, cols].astype(f32))

        def other(cols):
            zs[:, cols] = half(1 - h, cols).astype(bf16)

        tiles(p, other)
        flights[p, "z"] = start(remote(zs.at[:, span(p)], zr.at[:, span(p)], base + 7 * p + 6, across))

        def mine_too(cols):
            grad_out[:, cols] = half(h, cols)

        tiles(p, mine_too)

    def stage_four(p):
        flights[p, "z"].wait_recv()

        def finish(cols):
            grad_out[:, cols] = grad_out[:, cols] + zr[:, cols].astype(f32)

        tiles(p, finish)

    m_step = 128

    def gate_part(to_y):
        rows = pl.ds(pl.multiple_of(to_y * pair, pair), pair)
        cols = rows
        up_cols = pl.ds(pl.multiple_of(n_hidden + to_y * pair, pair), pair)

        def block(m, _):
            where = pl.ds(pl.multiple_of(m * m_step, m_step), m_step)
            proj = lax.dot_general(
                dout[where, :], shards[rows, :], (((1,), (1,)), ((), ())), preferred_element_type=f32
            )
            felt = hidden[where, cols].astype(f32) * proj
            total = gg_acc[where, :]
            for c in range(pair // 128):
                total = total + felt[:, c * 128 : (c + 1) * 128]
            gg_acc[where, :] = total
            grad_hidden = wcol[where, 0:1] * proj
            ggu_out[where, cols] = (grad_hidden * d_silu[where, cols]).astype(bf16)
            ggu_out[where, up_cols] = (grad_hidden * silu[where, cols]).astype(bf16)
            return _

        lax.fori_loop(0, n_slots // m_step, block, 0)

    gg_acc[...] = jnp.zeros_like(gg_acc)

    arrive(0)
    stage_one(0)
    ag_z = start(remote(shard(r), shard(r), 4, across))
    stage_two(0)
    arrive(1)
    stage_one(1)
    stage_three(0)
    stage_two(1)

    ag_z.wait_recv()
    ag_up3 = start(remote(shard(across[0]), shard(across[0]), 5, up))
    ag_down3 = start(remote(shard(across[0]), shard(across[0]), 6, down))
    stage_three(1)
    gate_part(y)
    up_other, down_other = across[0] + 2, across[0] + n_rep - 2
    up_other, down_other = lax.rem(up_other, n_rep), lax.rem(down_other, n_rep)
    ag_up3.wait_recv()
    ag_up4 = start(remote(half_shard(down_other, 0), half_shard(down_other, 0), 7, up))
    ag_down3.wait_recv()
    ag_down4 = start(remote(half_shard(up_other, 1), half_shard(up_other, 1), 8, down))
    gate_part(y_down)
    gate_part(y_up)
    stage_four(0)
    for copy in (ag_up2, ag_down2, ag_up4, ag_down4):
        copy.wait_recv()
    gate_part(y_far)

    gg_out[...] = jnp.broadcast_to(jnp.sum(gg_acc[...], axis=1, keepdims=True), gg_out.shape)

    def window(to):
        return gg_out.at[pl.ds(pl.multiple_of(to * SEND - 4 * lax.rem(to, 2), 8), 16)]

    gg_local = small(window, gg_in, 16, 1)
    stage_four(1)
    gg_local.wait()
    all_of(gg_in, 16, small_rsem.at[1]).wait()
    row = iota((n_ep * 16, 128), 0) - 4 * lax.rem(e, 2)
    back = gg_in[...]
    for k in range(TOPK):
        for b in range(n_tok // 128):
            cols = slice(b * 128, (b + 1) * 128)
            hit = row == pos16[k : k + 1, cols]
            gate_out[k : k + 1, cols] = jnp.sum(jnp.where(hit, back, 0.0), axis=0, keepdims=True)

    for copy in started:
        copy.wait_send()
    all_of(w_out, 16, small_ssem.at[0]).wait()
    all_of(gg_in, 16, small_ssem.at[1]).wait()
    for p in range(len(CHUNKS)):
        all_of(rows_out[p], msg, rows_ssem.at[p]).wait()


def outer(
    n_ep, n_rep,
    ids_ref, slots_ref, gates_ref, og_hbm, gu_hbm, master_hbm,
    ggu_out, gate_out, grad_out, *scratch,
):
    n = len(CHUNKS)
    og, gu, master, pick, unpick = scratch[:5]
    rows_out, rows_in = scratch[5 : 5 + n], scratch[5 + n : 5 + 2 * n]
    kernel(
        n_ep, n_rep, ids_ref, slots_ref, gates_ref, og_hbm, gu_hbm, master_hbm,
        ggu_out, gate_out, grad_out,
        og, gu, master, pick, unpick, rows_out, rows_in, *scratch[5 + 2 * n :],
    )


def exchange(n_ep, n_rep, ids, slots, gates, out_grad, gate_up, master):
    tokens, width = out_grad.shape
    n_slots, two_hidden = gate_up.shape
    n_hidden = two_hidden // 2
    part_rows = master.shape[0]
    pair = 2 * part_rows
    msg = PARTS * SEND
    f32, bf16 = jnp.float32, jnp.bfloat16
    n = len(CHUNKS)
    n_sems = 9 + 7 * n
    vmem = pl.BlockSpec(memory_space=pltpu.VMEM)
    hbm = pl.BlockSpec(memory_space=pl.ANY)
    rows = [pltpu.VMEM((n_ep * msg, size * 128), bf16) for size in CHUNKS]
    dma = pltpu.SemaphoreType.DMA
    return pl.pallas_call(
        functools.partial(outer, n_ep, n_rep),
        out_shape=(
            jax.ShapeDtypeStruct((n_slots, two_hidden), bf16),
            jax.ShapeDtypeStruct((TOPK, tokens), f32),
            jax.ShapeDtypeStruct((part_rows, width), f32),
        ),
        in_specs=[vmem, vmem, vmem, hbm, hbm, hbm],
        out_specs=(vmem, vmem, vmem),
        scratch_shapes=[
            pltpu.VMEM((tokens, width), bf16),
            pltpu.VMEM((n_slots, two_hidden), bf16),
            pltpu.VMEM((part_rows, width), f32),
            pltpu.VMEM((n_ep * msg, PARTS * tokens), bf16),
            pltpu.VMEM((PARTS * msg, PARTS * msg), bf16),
            *rows,
            *rows,
            pltpu.VMEM((n_ep * 16, 128), bf16),
            pltpu.VMEM((n_ep * 16, 128), bf16),
            pltpu.VMEM((n_slots, width), bf16),
            pltpu.VMEM((n_slots, 128), f32),
            pltpu.VMEM((n_slots, n_hidden), bf16),
            pltpu.VMEM((n_slots, n_hidden), f32),
            pltpu.VMEM((n_slots, n_hidden), f32),
            pltpu.VMEM((n_hidden, n_slots), bf16),
            pltpu.VMEM((n_hidden, width), bf16),
            pltpu.VMEM((pair, width), bf16),
            pltpu.VMEM((pair, width), bf16),
            pltpu.VMEM((pair, width), f32),
            pltpu.VMEM((pair, width), bf16),
            pltpu.VMEM((pair, width), bf16),
            pltpu.VMEM((pair, width), bf16),
            pltpu.VMEM((pair, width), bf16),
            pltpu.VMEM((pair, width), f32),
            pltpu.VMEM((part_rows, width), bf16),
            pltpu.VMEM((part_rows, width), bf16),
            pltpu.VMEM((n_slots, 128), f32),
            pltpu.VMEM((n_slots, 128), f32),
            pltpu.VMEM((n_ep * 16, 128), f32),
            dma((3,)),
            dma((n,)),
            dma((n,)),
            dma((2,)),
            dma((2,)),
            dma((2 + n,)),
            dma((n_sems,)),
            dma((n_sems,)),
        ],
        compiler_params=pltpu.CompilerParams(
            collective_id=0, has_side_effects=True, vmem_limit_bytes=60 * 1024 * 1024
        ),
        name="exchange",
    )(ids, slots, gates, out_grad, gate_up, master)


def solution(mesh):
    n_ep, n_rep = mesh.shape["ep"], mesh.shape["rep"]

    def per_device(out_grad, expert_ids, slots, gate_weights, saved_gate_up, master, moment1, moment2):
        grad_gate_up, gate_grad, grad = exchange(
            n_ep, n_rep, expert_ids.T, slots.T, gate_weights.T.astype(jnp.float32),
            out_grad, saved_gate_up[0, 0], master[0],
        )
        master_out, moment1_out, moment2_out = adamw(master, moment1, moment2, grad[None])
        return (grad_gate_up.reshape(saved_gate_up.shape), gate_grad.T, master_out, moment1_out, moment2_out)

    in_specs = (
        P(("rep", "ep"), None),
        P(("rep", "ep"), None),
        P(("rep", "ep"), None),
        P(("rep", "ep"), None),
        P("rep", "ep", None, None),
        P("ep", "rep", None),
        P("ep", "rep", None),
        P("ep", "rep", None),
    )
    out_specs = (
        P("rep", "ep", None, None),
        P(("rep", "ep"), None),
        P("ep", "rep", None),
        P("ep", "rep", None),
        P("ep", "rep", None),
    )
    return jax.shard_map(per_device, mesh=mesh, in_specs=in_specs, out_specs=out_specs, check_vma=False)
```

```python
import functools

import jax
import jax.numpy as jnp
from jax import lax
from jax.experimental import pallas as pl
from jax.experimental.pallas import tpu as pltpu
from jax.sharding import PartitionSpec as P

TOPK = 8
EXP_LOCAL = 8
SEND = 12
PARTS = 4
CHUNKS = (2, 2, 1, 1, 1)
TILE = 512
MESH = pl.DeviceIdType.MESH

beta_one = 0.9
beta_two = 0.95
learn_rate = 0.002
decay_rate = 0.1
adam_eps = 1e-08
adam_step = 50


def adamw(master, moment1, moment2, grad):
    m_new = beta_one * moment1.astype(jnp.float32) + (1.0 - beta_one) * grad
    v_new = beta_two * moment2.astype(jnp.float32) + (1.0 - beta_two) * grad * grad
    corr_one = 1.0 - beta_one**adam_step
    corr_two = 1.0 - beta_two**adam_step
    update = m_new / corr_one / (jnp.sqrt(v_new / corr_two) + adam_eps)
    master_new = master - learn_rate * (update + decay_rate * master)
    return (master_new, m_new.astype(jnp.bfloat16), v_new.astype(jnp.bfloat16))


def iota(shape, dim):
    return lax.broadcasted_iota(jnp.int32, shape, dim)


def div(x, by, top):
    shift = 20
    factor = (1 << shift) // by + 1
    assert all((v * factor) >> shift == v // by for v in range(top)) and top * factor < 2**31
    return (x * factor) >> shift


def kernel(
    n_ep, n_rep,
    ids_ref, slots_ref, gates_ref, og_hbm, gu_hbm, master_hbm, moment1_hbm, moment2_hbm,
    ggu_out, gate_out, master_out, moment1_out, moment2_out,
    og, gu, master, moment1, moment2, pick, unpick,
    rows_out, rows_in, w_out, w_in, dout, wcol,
    hidden, d_silu, silu, scaled_t, shards,
    s1, r1, keep, s2own, r2own, s2sum, r2sum, own, zs, zr,
    gg_acc, gg_out, gg_in,
    load_sem, store_sem, rows_ssem, rows_rsem, small_ssem, small_rsem, local_sem, ssem, rsem,
):
    f32, bf16 = jnp.float32, jnp.bfloat16
    r, e = lax.axis_index("rep"), lax.axis_index("ep")
    y, h = lax.div(r, 2), lax.rem(r, 2)
    n_y = n_rep // 2
    up = (lax.rem(r + 2, n_rep), e)
    down = (lax.rem(r + n_rep - 2, n_rep), e)
    across = (r + 1 - 2 * h, e)
    width = og.shape[1]
    part_rows = shards.shape[0] // n_rep
    pair = 2 * part_rows
    msg = PARTS * SEND
    offsets = [sum(CHUNKS[:i]) * PARTS * 128 for i in range(len(CHUNKS))]

    def peer(k):
        return lax.rem(e + k, n_ep)

    loads = [
        pltpu.make_async_copy(src, dst, load_sem.at[i])
        for i, (src, dst) in enumerate(
            (
                (og_hbm, og), (master_hbm, master), (gu_hbm, gu),
                (moment1_hbm, moment1), (moment2_hbm, moment2),
            )
        )
    ]
    for load in loads:
        load.start()

    barrier = pltpu.get_barrier_semaphore()

    def greet(k, _):
        pl.semaphore_signal(barrier, inc=1, device_id=(r, peer(k)), device_id_type=MESH)
        return _

    lax.fori_loop(1, n_ep, greet, 0)
    for other in (up, down, across):
        pl.semaphore_signal(barrier, inc=1, device_id=other, device_id_type=MESH)

    mine = pl.ds(pl.multiple_of(r * part_rows, part_rows), part_rows)
    loads[1].wait()

    def cast(t, _):
        cols = pl.ds(pl.multiple_of(t * TILE, TILE), TILE)
        shards[mine, cols] = master[:, cols].astype(bf16)
        return _

    lax.fori_loop(0, width // TILE, cast, 0)

    def remote(src, dst, i, other):
        return pltpu.make_async_remote_copy(
            src_ref=src, dst_ref=dst, send_sem=ssem.at[i], recv_sem=rsem.at[i],
            device_id=other, device_id_type=MESH,
        )

    pl.semaphore_wait(barrier, n_ep - 1 + 3)

    def shard(rep):
        return shards.at[pl.ds(pl.multiple_of(rep * part_rows, part_rows), part_rows)]

    def half_shard(rep, which):
        half = part_rows // 2
        return shards.at[pl.ds(pl.multiple_of(rep * part_rows + which * half, half), half)]

    started = []

    def start(copy):
        copy.start()
        started.append(copy)
        return copy

    ag_up = start(remote(shard(r), shard(r), 0, up))
    ag_down = start(remote(shard(r), shard(r), 1, down))
    ag_z = start(remote(shard(r), shard(r), 4, across))

    ids, slots = ids_ref[...], slots_ref[...]
    live = ((ids & (EXP_LOCAL - 1)) == 0) & (slots >= 0)
    expert = ids >> 3
    pos12 = jnp.where(live, expert * SEND + slots, -64)
    pos16 = jnp.where(live, expert * 16 + slots, -64)
    gates = gates_ref[...].astype(f32)
    n_tok = ids.shape[1]

    def pick_rows(g, _):
        row = iota((PARTS * msg, n_tok), 0)
        dest = div(row, msg, PARTS * msg)
        rest = row - dest * msg
        part = div(rest, SEND, msg)
        target = (dest + g * PARTS) * SEND + rest - part * SEND
        hit = target == pos12[0:1, :]
        for k in range(1, TOPK):
            hit = hit | (target == pos12[k : k + 1, :])
        for q in range(PARTS):
            one = jnp.where(hit & (part == q), 1.0, 0.0).astype(bf16)
            pick[pl.ds(pl.multiple_of(g * PARTS * msg, 16), PARTS * msg), q * n_tok : (q + 1) * n_tok] = one
        return _

    lax.fori_loop(0, n_ep // PARTS, pick_rows, 0)

    def small(src_of, dst, rows, sems):
        def send(k, _):
            to = peer(k)
            pltpu.make_async_remote_copy(
                src_ref=src_of(to), dst_ref=dst.at[pl.ds(pl.multiple_of(e * rows, rows), rows)],
                send_sem=small_ssem.at[sems], recv_sem=small_rsem.at[sems],
                device_id=(r, to), device_id_type=MESH,
            ).start()
            return _

        lax.fori_loop(1, n_ep, send, 0)
        copy = pltpu.make_async_copy(
            src_of(e), dst.at[pl.ds(pl.multiple_of(e * rows, rows), rows)], local_sem.at[sems]
        )
        copy.start()
        return copy

    def all_of(ref, rows, sem):
        part = ref.at[pl.ds(0, (n_ep - 1) * rows)]
        return pltpu.make_async_copy(part, part, sem)

    def weight_rows(b, _):
        row = iota((64, n_tok), 0) + b * 64
        total = jnp.zeros((64, n_tok), f32)
        for k in range(TOPK):
            total += jnp.where(row == pos16[k : k + 1, :], gates[k : k + 1, :], 0.0)
        column = jnp.sum(total, axis=1, keepdims=True)
        w_out[pl.ds(pl.multiple_of(b * 64, 64), 64), :] = jnp.broadcast_to(column, (64, 128)).astype(bf16)
        return _

    lax.fori_loop(0, n_ep * 16 // 64, weight_rows, 0)
    w_local = small(lambda to: w_out.at[pl.ds(pl.multiple_of(to * 16, 16), 16)], w_in, 16, 0)

    loads[0].wait()
    rows_local = []
    for p, size in enumerate(CHUNKS):
        wide = size * 128
        out, into = rows_out[p], rows_in[p]

        def gather(g, _, out=out, wide=wide, p=p):
            where = pl.ds(pl.multiple_of(g * PARTS * msg, 16), PARTS * msg)
            total = jnp.zeros((PARTS * msg, wide), f32)
            for q in range(PARTS):
                total += jnp.dot(
                    pick[where, q * n_tok : (q + 1) * n_tok],
                    og[:, offsets[p] + q * wide : offsets[p] + (q + 1) * wide],
                    preferred_element_type=f32,
                )
            out[where, :] = total.astype(bf16)
            return _

        lax.fori_loop(0, n_ep // PARTS, gather, 0)

        def block(ref, i):
            return ref.at[pl.ds(pl.multiple_of(i * msg, 16), msg)]

        def send(k, _, out=out, into=into, p=p):
            to = peer(k)
            pltpu.make_async_remote_copy(
                src_ref=block(out, to), dst_ref=block(into, e),
                send_sem=rows_ssem.at[p], recv_sem=rows_rsem.at[p],
                device_id=(r, to), device_id_type=MESH,
            ).start()
            return _

        lax.fori_loop(1, n_ep, send, 0)
        copy = pltpu.make_async_copy(block(out, e), block(into, e), local_sem.at[2 + p])
        copy.start()
        rows_local.append(copy)

    loads[2].wait()
    n_hidden = hidden.shape[1]
    step = 128

    def activation(t, _):
        cols = pl.ds(pl.multiple_of(t * step, step), step)
        up_cols = pl.ds(pl.multiple_of(n_hidden + t * step, step), step)
        gate, lift = gu[:, cols].astype(f32), gu[:, up_cols].astype(f32)
        sig = jax.nn.sigmoid(gate)
        act = gate * sig
        hidden[:, cols] = (act * lift).astype(bf16)
        silu[:, cols] = act
        d_silu[:, cols] = lift * sig * (1.0 + gate * (1.0 - sig))
        return _

    lax.fori_loop(0, n_hidden // step, activation, 0)
    side = PARTS * msg
    row = iota((side, side), 0)
    part = div(row, msg, side)
    rest = row - part * msg
    dest = div(rest, SEND, msg)
    unpick[...] = jnp.where(
        iota((side, side), 1) == dest * msg + part * SEND + rest - dest * SEND, 1.0, 0.0
    ).astype(bf16)

    ag_up.wait_recv()
    ag_up2 = start(remote(half_shard(down[0], 0), half_shard(down[0], 0), 2, up))
    ag_down.wait_recv()
    ag_down2 = start(remote(half_shard(up[0], 1), half_shard(up[0], 1), 3, down))

    w_local.wait()
    all_of(w_in, 16, small_rsem.at[0]).wait()
    n_slots = n_ep * SEND
    row = iota((n_slots, n_ep * 16), 0)
    dest = div(row, SEND, n_slots)
    order = jnp.where(iota(row.shape, 1) == row + dest * (16 - SEND), 1.0, 0.0).astype(bf16)
    wcol[...] = jnp.dot(order, w_in[...], preferred_element_type=f32)

    def scale(t, _):
        cols = pl.ds(pl.multiple_of(t * step, step), step)
        value = wcol[...] * hidden[:, cols].astype(f32)
        scaled_t[cols, :] = value.astype(bf16).astype(f32).T.astype(bf16)
        return _

    lax.fori_loop(0, n_hidden // step, scale, 0)

    def span(p):
        return pl.ds(offsets[p], CHUNKS[p] * PARTS * 128)

    def tiles(p, body):
        def one(t, _):
            body(pl.ds(pl.multiple_of(offsets[p] + t * TILE, TILE), TILE))
            return _

        lax.fori_loop(0, CHUNKS[p] * PARTS * 128 // TILE, one, 0)

    def arrive(p):
        wide = CHUNKS[p] * 128
        rows_local[p].wait()
        all_of(rows_in[p], msg, rows_rsem.at[p]).wait()

        def restore(g, _):
            got = jnp.dot(
                unpick[...],
                rows_in[p][pl.ds(pl.multiple_of(g * side, 16), side), :],
                preferred_element_type=f32,
            ).astype(bf16)
            for q in range(PARTS):
                dout[pl.ds(pl.multiple_of(g * msg, 16), msg), offsets[p] + q * wide : offsets[p] + (q + 1) * wide] = (
                    got[q * msg : (q + 1) * msg]
                )
            return _

        lax.fori_loop(0, n_ep // PARTS, restore, 0)

    def product(to_y, cols):
        rows = pl.ds(pl.multiple_of(to_y * pair, pair), pair)
        return jnp.dot(scaled_t[rows, :], dout[:, cols], preferred_element_type=f32)

    y_up, y_down, y_far = lax.rem(y + 1, n_y), lax.rem(y + n_y - 1, n_y), lax.rem(y + 2, n_y)
    first, second = pl.ds(0, part_rows), pl.ds(part_rows, part_rows)
    base = 9
    flights = {}

    def stage_one(p):
        def far(cols):
            s1[:, cols] = product(y_far, cols).astype(bf16)

        tiles(p, far)
        i = base + 7 * p
        flights[p, "a"] = start(remote(s1.at[first, span(p)], r1.at[first, span(p)], i, up))
        flights[p, "b"] = start(remote(s1.at[second, span(p)], r1.at[second, span(p)], i + 1, down))

        def near(cols):
            got = product(y_up, cols)
            keep[first, cols] = got[:part_rows]
            s2own[second, cols] = got[part_rows:].astype(bf16)
            got = product(y_down, cols)
            s2own[first, cols] = got[:part_rows].astype(bf16)
            keep[second, cols] = got[part_rows:]

        tiles(p, near)
        flights[p, "own_b"] = start(remote(s2own.at[second, span(p)], r2own.at[second, span(p)], i + 2, up))
        flights[p, "own_a"] = start(remote(s2own.at[first, span(p)], r2own.at[first, span(p)], i + 3, down))

        def here(cols):
            own[:, cols] = product(y, cols)

        tiles(p, here)

    def stage_two(p):
        i = base + 7 * p
        for name, rows, other, j in (("a", first, up, i + 4), ("b", second, down, i + 5)):
            flights[p, name].wait_recv()

            def add(cols, rows=rows):
                s2sum[rows, cols] = (keep[rows, cols] + r1[rows, cols].astype(f32)).astype(bf16)

            tiles(p, add)
            flights[p, "sum_" + name] = start(remote(s2sum.at[rows, span(p)], r2sum.at[rows, span(p)], j, other))

    def half(which, cols):
        rows = pl.ds(pl.multiple_of(which * part_rows, part_rows), part_rows)
        return own[rows, cols] + (r2own[rows, cols].astype(f32) + r2sum[rows, cols].astype(f32))

    def stage_three(p):
        for name in ("own_a", "own_b", "sum_a", "sum_b"):
            flights[p, name].wait_recv()

        def other(cols):
            zs[:, cols] = half(1 - h, cols).astype(bf16)

        tiles(p, other)
        flights[p, "z"] = start(remote(zs.at[:, span(p)], zr.at[:, span(p)], base + 7 * p + 6, across))

    stores = []

    def store(src, dst):
        copy = pltpu.make_async_copy(src, dst, store_sem.at[len(stores)])
        copy.start()
        stores.append(copy)

    def stage_four(p):
        flights[p, "z"].wait_recv()

        def finish(cols):
            grad = half(h, cols) + zr[:, cols].astype(f32)
            master[:, cols], moment1[:, cols], moment2[:, cols] = adamw(
                master[:, cols], moment1[:, cols], moment2[:, cols], grad
            )

        tiles(p, finish)
        for src, dst in ((master, master_out), (moment1, moment1_out), (moment2, moment2_out)):
            store(src.at[:, span(p)], dst.at[:, span(p)])

    m_step = 128

    def gate_part(to_y):
        rows = pl.ds(pl.multiple_of(to_y * pair, pair), pair)
        cols = rows
        up_cols = pl.ds(pl.multiple_of(n_hidden + to_y * pair, pair), pair)

        def block(m, _):
            where = pl.ds(pl.multiple_of(m * m_step, m_step), m_step)
            proj = lax.dot_general(
                dout[where, :], shards[rows, :], (((1,), (1,)), ((), ())), preferred_element_type=f32
            )
            felt = hidden[where, cols].astype(f32) * proj
            total = gg_acc[where, :]
            for c in range(pair // 128):
                total = total + felt[:, c * 128 : (c + 1) * 128]
            gg_acc[where, :] = total
            grad_hidden = wcol[where, 0:1] * proj
            gu[where, cols] = (grad_hidden * d_silu[where, cols]).astype(bf16)
            gu[where, up_cols] = (grad_hidden * silu[where, cols]).astype(bf16)
            return _

        lax.fori_loop(0, n_slots // m_step, block, 0)

    gg_acc[...] = jnp.zeros_like(gg_acc)

    up_other, down_other = lax.rem(across[0] + 2, n_rep), lax.rem(across[0] + n_rep - 2, n_rep)
    ag_z.wait_recv()
    ag_up3 = start(remote(shard(across[0]), shard(across[0]), 5, up))
    ag_down3 = start(remote(shard(across[0]), shard(across[0]), 6, down))
    ag_up3.wait_recv()
    ag_up4 = start(remote(half_shard(down_other, 0), half_shard(down_other, 0), 7, up))
    ag_down3.wait_recv()
    ag_down4 = start(remote(half_shard(up_other, 1), half_shard(up_other, 1), 8, down))

    last = len(CHUNKS) - 1
    for p in range(last + 1):
        arrive(p)
        stage_one(p)
        if p:
            stage_three(p - 1)
        stage_two(p)
    gate_part(y)
    gate_part(y_down)
    gate_part(y_up)
    for copy in (ag_up2, ag_down2, ag_up4, ag_down4):
        copy.wait_recv()
    gate_part(y_far)
    store(gu, ggu_out)
    stage_three(last)

    gg_out[...] = jnp.broadcast_to(jnp.sum(gg_acc[...], axis=1, keepdims=True), gg_out.shape)

    def window(to):
        return gg_out.at[pl.ds(pl.multiple_of(to * SEND - 4 * lax.rem(to, 2), 8), 16)]

    gg_local = small(window, gg_in, 16, 1)
    loads[3].wait()
    loads[4].wait()
    for p in range(last + 1):
        stage_four(p)
    gg_local.wait()
    all_of(gg_in, 16, small_rsem.at[1]).wait()
    row = iota((n_ep * 16, 128), 0) - 4 * lax.rem(e, 2)
    back = gg_in[...]
    for k in range(TOPK):
        for b in range(n_tok // 128):
            cols = slice(b * 128, (b + 1) * 128)
            hit = row == pos16[k : k + 1, cols]
            gate_out[k : k + 1, cols] = jnp.sum(jnp.where(hit, back, 0.0), axis=0, keepdims=True)

    for copy in stores:
        copy.wait()
    for copy in started:
        copy.wait_send()
    all_of(w_out, 16, small_ssem.at[0]).wait()
    all_of(gg_in, 16, small_ssem.at[1]).wait()
    for p in range(len(CHUNKS)):
        all_of(rows_out[p], msg, rows_ssem.at[p]).wait()


def outer(
    n_ep, n_rep,
    ids_ref, slots_ref, gates_ref, og_hbm, gu_hbm, master_hbm, moment1_hbm, moment2_hbm,
    ggu_out, gate_out, master_out, moment1_out, moment2_out, *scratch,
):
    n = len(CHUNKS)
    rows_out, rows_in = scratch[7 : 7 + n], scratch[7 + n : 7 + 2 * n]
    kernel(
        n_ep, n_rep, ids_ref, slots_ref, gates_ref, og_hbm, gu_hbm, master_hbm, moment1_hbm, moment2_hbm,
        ggu_out, gate_out, master_out, moment1_out, moment2_out,
        *scratch[:7], rows_out, rows_in, *scratch[7 + 2 * n :],
    )


def exchange(n_ep, n_rep, ids, slots, gates, out_grad, gate_up, master, moment1, moment2):
    tokens, width = out_grad.shape
    n_slots, two_hidden = gate_up.shape
    n_hidden = two_hidden // 2
    part_rows = master.shape[0]
    pair = 2 * part_rows
    msg = PARTS * SEND
    f32, bf16 = jnp.float32, jnp.bfloat16
    n = len(CHUNKS)
    n_sems = 9 + 7 * n
    vmem = pl.BlockSpec(memory_space=pltpu.VMEM)
    hbm = pl.BlockSpec(memory_space=pl.ANY)
    rows = [pltpu.VMEM((n_ep * msg, size * 128), bf16) for size in CHUNKS]
    dma = pltpu.SemaphoreType.DMA
    return pl.pallas_call(
        functools.partial(outer, n_ep, n_rep),
        out_shape=(
            jax.ShapeDtypeStruct((n_slots, two_hidden), bf16),
            jax.ShapeDtypeStruct((TOPK, tokens), f32),
            jax.ShapeDtypeStruct((part_rows, width), f32),
            jax.ShapeDtypeStruct((part_rows, width), bf16),
            jax.ShapeDtypeStruct((part_rows, width), bf16),
        ),
        in_specs=[vmem, vmem, vmem, hbm, hbm, hbm, hbm, hbm],
        out_specs=(hbm, vmem, hbm, hbm, hbm),
        scratch_shapes=[
            pltpu.VMEM((tokens, width), bf16),
            pltpu.VMEM((n_slots, two_hidden), bf16),
            pltpu.VMEM((part_rows, width), f32),
            pltpu.VMEM((part_rows, width), bf16),
            pltpu.VMEM((part_rows, width), bf16),
            pltpu.VMEM((n_ep * msg, PARTS * tokens), bf16),
            pltpu.VMEM((PARTS * msg, PARTS * msg), bf16),
            *rows,
            *rows,
            pltpu.VMEM((n_ep * 16, 128), bf16),
            pltpu.VMEM((n_ep * 16, 128), bf16),
            pltpu.VMEM((n_slots, width), bf16),
            pltpu.VMEM((n_slots, 128), f32),
            pltpu.VMEM((n_slots, n_hidden), bf16),
            pltpu.VMEM((n_slots, n_hidden), f32),
            pltpu.VMEM((n_slots, n_hidden), f32),
            pltpu.VMEM((n_hidden, n_slots), bf16),
            pltpu.VMEM((n_hidden, width), bf16),
            pltpu.VMEM((pair, width), bf16),
            pltpu.VMEM((pair, width), bf16),
            pltpu.VMEM((pair, width), f32),
            pltpu.VMEM((pair, width), bf16),
            pltpu.VMEM((pair, width), bf16),
            pltpu.VMEM((pair, width), bf16),
            pltpu.VMEM((pair, width), bf16),
            pltpu.VMEM((pair, width), f32),
            pltpu.VMEM((part_rows, width), bf16),
            pltpu.VMEM((part_rows, width), bf16),
            pltpu.VMEM((n_slots, 128), f32),
            pltpu.VMEM((n_slots, 128), f32),
            pltpu.VMEM((n_ep * 16, 128), f32),
            dma((5,)),
            dma((1 + 3 * n,)),
            dma((n,)),
            dma((n,)),
            dma((2,)),
            dma((2,)),
            dma((2 + n,)),
            dma((n_sems,)),
            dma((n_sems,)),
        ],
        compiler_params=pltpu.CompilerParams(
            collective_id=0, has_side_effects=True, vmem_limit_bytes=60 * 1024 * 1024
        ),
        name="exchange",
    )(ids, slots, gates, out_grad, gate_up, master, moment1, moment2)


def hand_over(n, *refs):
    given, taken, held = refs[:n], refs[n : 2 * n], refs[2 * n : 3 * n]
    get_sem, put_sem = refs[3 * n :]
    gets = [pltpu.make_async_copy(given[i], held[i], get_sem.at[i]) for i in range(n)]
    puts = [pltpu.make_async_copy(held[i], taken[i], put_sem.at[i]) for i in range(n)]
    for get in gets:
        get.start()
    for get, put in zip(gets, puts):
        get.wait()
        put.start()
    for put in puts:
        put.wait()


def results(*arrays):
    n = len(arrays)
    hbm = pl.BlockSpec(memory_space=pl.ANY)
    sems = pltpu.SemaphoreType.DMA((n,))
    return pl.pallas_call(
        functools.partial(hand_over, n),
        out_shape=tuple(jax.ShapeDtypeStruct(a.shape, a.dtype) for a in arrays),
        in_specs=[hbm] * n,
        out_specs=(hbm,) * n,
        scratch_shapes=[*(pltpu.VMEM(a.shape, a.dtype) for a in arrays), sems, sems],
        compiler_params=pltpu.CompilerParams(vmem_limit_bytes=62 * 1024 * 1024),
        name="results",
    )(*arrays)


def solution(mesh):
    n_ep, n_rep = mesh.shape["ep"], mesh.shape["rep"]

    def per_device(out_grad, expert_ids, slots, gate_weights, saved_gate_up, master, moment1, moment2):
        grad_gate_up, gate_grad, *state = results(
            *exchange(
                n_ep, n_rep, expert_ids.T, slots.T, gate_weights.T,
                out_grad, saved_gate_up[0, 0], master[0], moment1[0], moment2[0],
            )
        )
        return (grad_gate_up.reshape(saved_gate_up.shape), gate_grad.T, *(part[None] for part in state))

    in_specs = (
        P(("rep", "ep"), None),
        P(("rep", "ep"), None),
        P(("rep", "ep"), None),
        P(("rep", "ep"), None),
        P("rep", "ep", None, None),
        P("ep", "rep", None),
        P("ep", "rep", None),
        P("ep", "rep", None),
    )
    out_specs = (
        P("rep", "ep", None, None),
        P(("rep", "ep"), None),
        P("ep", "rep", None),
        P("ep", "rep", None),
        P("ep", "rep", None),
    )
    return jax.shard_map(per_device, mesh=mesh, in_specs=in_specs, out_specs=out_specs, check_vma=False)
```

```python
import functools

import jax
import jax.numpy as jnp
from jax import lax
from jax.experimental import pallas as pl
from jax.experimental.pallas import tpu as pltpu
from jax.sharding import PartitionSpec as P

TOPK = 8
EXP_LOCAL = 8
SEND = 12
PARTS = 4
CHUNKS = (2, 2, 1, 1, 1)
TILE = 512
MESH = pl.DeviceIdType.MESH

beta_one = 0.9
beta_two = 0.95
learn_rate = 0.002
decay_rate = 0.1
adam_eps = 1e-08
adam_step = 50


def adamw(master, moment1, moment2, grad):
    m_new = beta_one * moment1.astype(jnp.float32) + (1.0 - beta_one) * grad
    v_new = beta_two * moment2.astype(jnp.float32) + (1.0 - beta_two) * grad * grad
    corr_one = 1.0 - beta_one**adam_step
    corr_two = 1.0 - beta_two**adam_step
    update = m_new / corr_one / (jnp.sqrt(v_new / corr_two) + adam_eps)
    master_new = master - learn_rate * (update + decay_rate * master)
    return (master_new, m_new.astype(jnp.bfloat16), v_new.astype(jnp.bfloat16))


def iota(shape, dim):
    return lax.broadcasted_iota(jnp.int32, shape, dim)


def div(x, by, top):
    shift = 20
    factor = (1 << shift) // by + 1
    assert all((v * factor) >> shift == v // by for v in range(top)) and top * factor < 2**31
    return (x * factor) >> shift


def kernel(
    n_ep, n_rep,
    ids_ref, slots_ref, gates_ref, og_hbm, gu_hbm, master_hbm, moment1_hbm, moment2_hbm,
    ggu_out, gate_out, master_out, moment1_out, moment2_out,
    og, gu, master, moment1, moment2, pick, unpick,
    rows_out, rows_in, w_out, w_in, dout, wcol,
    hidden, d_silu, silu, proj, scaled_t, shards,
    s1, r1, keep, s2own, r2own, s2sum, r2sum, own, zs, zr,
    gg_acc, gg_out, gg_in,
    load_sem, store_sem, rows_ssem, rows_rsem, small_ssem, small_rsem, local_sem, ssem, rsem,
):
    f32, bf16 = jnp.float32, jnp.bfloat16
    r, e = lax.axis_index("rep"), lax.axis_index("ep")
    y, h = lax.div(r, 2), lax.rem(r, 2)
    n_y = n_rep // 2
    up = (lax.rem(r + 2, n_rep), e)
    down = (lax.rem(r + n_rep - 2, n_rep), e)
    across = (r + 1 - 2 * h, e)
    width = og.shape[1]
    part_rows = shards.shape[0] // n_rep
    pair = 2 * part_rows
    msg = PARTS * SEND
    offsets = [sum(CHUNKS[:i]) * PARTS * 128 for i in range(len(CHUNKS))]

    def peer(k):
        return lax.rem(e + k, n_ep)

    loads = [
        pltpu.make_async_copy(src, dst, load_sem.at[i])
        for i, (src, dst) in enumerate(
            (
                (og_hbm, og), (master_hbm, master), (gu_hbm, gu),
                (moment1_hbm, moment1), (moment2_hbm, moment2),
            )
        )
    ]
    loads[1].start()

    barrier = pltpu.get_barrier_semaphore()

    def greet(k, _):
        pl.semaphore_signal(barrier, inc=1, device_id=(r, peer(k)), device_id_type=MESH)
        return _

    lax.fori_loop(1, n_ep, greet, 0)
    for other in (up, down, across):
        pl.semaphore_signal(barrier, inc=1, device_id=other, device_id_type=MESH)

    mine = pl.ds(pl.multiple_of(r * part_rows, part_rows), part_rows)
    loads[1].wait()

    def cast(t, _):
        cols = pl.ds(pl.multiple_of(t * TILE, TILE), TILE)
        shards[mine, cols] = master[:, cols].astype(bf16)
        return _

    lax.fori_loop(0, width // TILE, cast, 0)

    def remote(src, dst, i, other):
        return pltpu.make_async_remote_copy(
            src_ref=src, dst_ref=dst, send_sem=ssem.at[i], recv_sem=rsem.at[i],
            device_id=other, device_id_type=MESH,
        )

    for i in (0, 2, 3, 4):
        loads[i].start()
    pl.semaphore_wait(barrier, n_ep - 1 + 3)

    def shard(rep):
        return shards.at[pl.ds(pl.multiple_of(rep * part_rows, part_rows), part_rows)]

    def half_shard(rep, which):
        half = part_rows // 2
        return shards.at[pl.ds(pl.multiple_of(rep * part_rows + which * half, half), half)]

    started = []

    def start(copy):
        copy.start()
        started.append(copy)
        return copy

    ag_up = start(remote(shard(r), shard(r), 0, up))
    ag_down = start(remote(shard(r), shard(r), 1, down))
    ag_z = start(remote(shard(r), shard(r), 4, across))

    ids, slots = ids_ref[...], slots_ref[...]
    live = ((ids & (EXP_LOCAL - 1)) == 0) & (slots >= 0)
    expert = ids >> 3
    pos12 = jnp.where(live, expert * SEND + slots, -64)
    pos16 = jnp.where(live, expert * 16 + slots, -64)
    gates = gates_ref[...].astype(f32)
    n_tok = ids.shape[1]

    def pick_rows(g, _):
        row = iota((PARTS * msg, n_tok), 0)
        dest = div(row, msg, PARTS * msg)
        rest = row - dest * msg
        part = div(rest, SEND, msg)
        target = (dest + g * PARTS) * SEND + rest - part * SEND
        hit = target == pos12[0:1, :]
        for k in range(1, TOPK):
            hit = hit | (target == pos12[k : k + 1, :])
        for q in range(PARTS):
            one = jnp.where(hit & (part == q), 1.0, 0.0).astype(bf16)
            pick[pl.ds(pl.multiple_of(g * PARTS * msg, 16), PARTS * msg), q * n_tok : (q + 1) * n_tok] = one
        return _

    lax.fori_loop(0, n_ep // PARTS, pick_rows, 0)

    def small(src_of, dst, rows, sems):
        def send(k, _):
            to = peer(k)
            pltpu.make_async_remote_copy(
                src_ref=src_of(to), dst_ref=dst.at[pl.ds(pl.multiple_of(e * rows, rows), rows)],
                send_sem=small_ssem.at[sems], recv_sem=small_rsem.at[sems],
                device_id=(r, to), device_id_type=MESH,
            ).start()
            return _

        lax.fori_loop(1, n_ep, send, 0)
        copy = pltpu.make_async_copy(
            src_of(e), dst.at[pl.ds(pl.multiple_of(e * rows, rows), rows)], local_sem.at[sems]
        )
        copy.start()
        return copy

    def all_of(ref, rows, sem):
        part = ref.at[pl.ds(0, (n_ep - 1) * rows)]
        return pltpu.make_async_copy(part, part, sem)

    def weight_rows(b, _):
        row = iota((64, n_tok), 0) + b * 64
        total = jnp.zeros((64, n_tok), f32)
        for k in range(TOPK):
            total += jnp.where(row == pos16[k : k + 1, :], gates[k : k + 1, :], 0.0)
        column = jnp.sum(total, axis=1, keepdims=True)
        w_out[pl.ds(pl.multiple_of(b * 64, 64), 64), :] = jnp.broadcast_to(column, (64, 128)).astype(bf16)
        return _

    lax.fori_loop(0, n_ep * 16 // 64, weight_rows, 0)
    w_local = small(lambda to: w_out.at[pl.ds(pl.multiple_of(to * 16, 16), 16)], w_in, 16, 0)

    loads[0].wait()
    rows_local = []
    for p, size in enumerate(CHUNKS):
        wide = size * 128
        out, into = rows_out[p], rows_in[p]

        def gather(g, _, out=out, wide=wide, p=p):
            where = pl.ds(pl.multiple_of(g * PARTS * msg, 16), PARTS * msg)
            total = jnp.zeros((PARTS * msg, wide), f32)
            for q in range(PARTS):
                total += jnp.dot(
                    pick[where, q * n_tok : (q + 1) * n_tok],
                    og[:, offsets[p] + q * wide : offsets[p] + (q + 1) * wide],
                    preferred_element_type=f32,
                )
            out[where, :] = total.astype(bf16)
            return _

        lax.fori_loop(0, n_ep // PARTS, gather, 0)

        def block(ref, i):
            return ref.at[pl.ds(pl.multiple_of(i * msg, 16), msg)]

        def send(k, _, out=out, into=into, p=p):
            to = peer(k)
            pltpu.make_async_remote_copy(
                src_ref=block(out, to), dst_ref=block(into, e),
                send_sem=rows_ssem.at[p], recv_sem=rows_rsem.at[p],
                device_id=(r, to), device_id_type=MESH,
            ).start()
            return _

        lax.fori_loop(1, n_ep, send, 0)
        copy = pltpu.make_async_copy(block(out, e), block(into, e), local_sem.at[2 + p])
        copy.start()
        rows_local.append(copy)

    loads[2].wait()
    n_hidden = hidden.shape[1]
    step = 128

    def activation(t, _):
        cols = pl.ds(pl.multiple_of(t * step, step), step)
        up_cols = pl.ds(pl.multiple_of(n_hidden + t * step, step), step)
        gate, lift = gu[:, cols].astype(f32), gu[:, up_cols].astype(f32)
        sig = jax.nn.sigmoid(gate)
        act = gate * sig
        hidden[:, cols] = (act * lift).astype(bf16)
        silu[:, cols] = act
        d_silu[:, cols] = lift * sig * (1.0 + gate * (1.0 - sig))
        return _

    lax.fori_loop(0, n_hidden // step, activation, 0)
    side = PARTS * msg
    row = iota((side, side), 0)
    part = div(row, msg, side)
    rest = row - part * msg
    dest = div(rest, SEND, msg)
    unpick[...] = jnp.where(
        iota((side, side), 1) == dest * msg + part * SEND + rest - dest * SEND, 1.0, 0.0
    ).astype(bf16)

    ag_up.wait_recv()
    ag_up2 = start(remote(half_shard(down[0], 0), half_shard(down[0], 0), 2, up))
    ag_down.wait_recv()
    ag_down2 = start(remote(half_shard(up[0], 1), half_shard(up[0], 1), 3, down))

    w_local.wait()
    all_of(w_in, 16, small_rsem.at[0]).wait()
    n_slots = n_ep * SEND
    row = iota((n_slots, n_ep * 16), 0)
    dest = div(row, SEND, n_slots)
    order = jnp.where(iota(row.shape, 1) == row + dest * (16 - SEND), 1.0, 0.0).astype(bf16)
    wcol[...] = jnp.dot(order, w_in[...], preferred_element_type=f32)

    def scale(t, _):
        cols = pl.ds(pl.multiple_of(t * step, step), step)
        value = wcol[...] * hidden[:, cols].astype(f32)
        scaled_t[cols, :] = value.astype(bf16).astype(f32).T.astype(bf16)
        return _

    lax.fori_loop(0, n_hidden // step, scale, 0)

    def span(p):
        return pl.ds(offsets[p], CHUNKS[p] * PARTS * 128)

    def tiles(p, body):
        def one(t, _):
            body(pl.ds(pl.multiple_of(offsets[p] + t * TILE, TILE), TILE))
            return _

        lax.fori_loop(0, CHUNKS[p] * PARTS * 128 // TILE, one, 0)

    def arrive(p):
        wide = CHUNKS[p] * 128
        rows_local[p].wait()
        all_of(rows_in[p], msg, rows_rsem.at[p]).wait()

        def restore(g, _):
            got = jnp.dot(
                unpick[...],
                rows_in[p][pl.ds(pl.multiple_of(g * side, 16), side), :],
                preferred_element_type=f32,
            ).astype(bf16)
            for q in range(PARTS):
                dout[pl.ds(pl.multiple_of(g * msg, 16), msg), offsets[p] + q * wide : offsets[p] + (q + 1) * wide] = (
                    got[q * msg : (q + 1) * msg]
                )
            return _

        lax.fori_loop(0, n_ep // PARTS, restore, 0)

    def product(to_y, cols):
        rows = pl.ds(pl.multiple_of(to_y * pair, pair), pair)
        return jnp.dot(scaled_t[rows, :], dout[:, cols], preferred_element_type=f32)

    y_up, y_down, y_far = lax.rem(y + 1, n_y), lax.rem(y + n_y - 1, n_y), lax.rem(y + 2, n_y)
    first, second = pl.ds(0, part_rows), pl.ds(part_rows, part_rows)
    base = 9
    flights = {}

    def stage_one(p):
        def far(cols):
            s1[:, cols] = product(y_far, cols).astype(bf16)

        tiles(p, far)
        i = base + 7 * p
        flights[p, "a"] = start(remote(s1.at[first, span(p)], r1.at[first, span(p)], i, up))
        flights[p, "b"] = start(remote(s1.at[second, span(p)], r1.at[second, span(p)], i + 1, down))

        def near(cols):
            got = product(y_up, cols)
            keep[first, cols] = got[:part_rows]
            s2own[second, cols] = got[part_rows:].astype(bf16)
            got = product(y_down, cols)
            s2own[first, cols] = got[:part_rows].astype(bf16)
            keep[second, cols] = got[part_rows:]

        tiles(p, near)
        flights[p, "own_b"] = start(remote(s2own.at[second, span(p)], r2own.at[second, span(p)], i + 2, up))
        flights[p, "own_a"] = start(remote(s2own.at[first, span(p)], r2own.at[first, span(p)], i + 3, down))

        def here(cols):
            own[:, cols] = product(y, cols)

        tiles(p, here)

    def stage_two(p):
        i = base + 7 * p
        for name, rows, other, j in (("a", first, up, i + 4), ("b", second, down, i + 5)):
            flights[p, name].wait_recv()

            def add(cols, rows=rows):
                s2sum[rows, cols] = (keep[rows, cols] + r1[rows, cols].astype(f32)).astype(bf16)

            tiles(p, add)
            flights[p, "sum_" + name] = start(remote(s2sum.at[rows, span(p)], r2sum.at[rows, span(p)], j, other))

    def half(which, cols):
        rows = pl.ds(pl.multiple_of(which * part_rows, part_rows), part_rows)
        return own[rows, cols] + (r2own[rows, cols].astype(f32) + r2sum[rows, cols].astype(f32))

    def stage_three(p):
        for name in ("own_a", "own_b", "sum_a", "sum_b"):
            flights[p, name].wait_recv()

        def other(cols):
            zs[:, cols] = half(1 - h, cols).astype(bf16)

        tiles(p, other)
        flights[p, "z"] = start(remote(zs.at[:, span(p)], zr.at[:, span(p)], base + 7 * p + 6, across))

    stores = []

    def store(src, dst):
        copy = pltpu.make_async_copy(src, dst, store_sem.at[len(stores)])
        copy.start()
        stores.append(copy)

    def stage_four(p):
        flights[p, "z"].wait_recv()

        def finish(cols):
            grad = half(h, cols) + zr[:, cols].astype(f32)
            master[:, cols], moment1[:, cols], moment2[:, cols] = adamw(
                master[:, cols], moment1[:, cols], moment2[:, cols], grad
            )

        tiles(p, finish)
        for src, dst in ((master, master_out), (moment1, moment1_out), (moment2, moment2_out)):
            store(src.at[:, span(p)], dst.at[:, span(p)])

    def project(p):
        def block(b, _):
            rows = pl.ds(pl.multiple_of(b * pair, pair), pair)
            got = lax.dot_general(
                dout[:, span(p)], shards[rows, span(p)], (((1,), (1,)), ((), ())), preferred_element_type=f32
            )
            proj[:, rows] = got if p == 0 else proj[:, rows] + got
            return _

        lax.fori_loop(0, n_hidden // pair, block, 0)

    def gate_finish():
        def block(t, _):
            cols = pl.ds(pl.multiple_of(t * step, step), step)
            up_cols = pl.ds(pl.multiple_of(n_hidden + t * step, step), step)
            value = proj[:, cols]
            gg_acc[...] += hidden[:, cols].astype(f32) * value
            grad_hidden = wcol[...] * value
            gu[:, cols] = (grad_hidden * d_silu[:, cols]).astype(bf16)
            gu[:, up_cols] = (grad_hidden * silu[:, cols]).astype(bf16)
            return _

        lax.fori_loop(0, n_hidden // step, block, 0)

    gg_acc[...] = jnp.zeros_like(gg_acc)

    up_other, down_other = lax.rem(across[0] + 2, n_rep), lax.rem(across[0] + n_rep - 2, n_rep)
    ag_z.wait_recv()
    ag_up3 = start(remote(shard(across[0]), shard(across[0]), 5, up))
    ag_down3 = start(remote(shard(across[0]), shard(across[0]), 6, down))
    ag_up3.wait_recv()
    ag_up4 = start(remote(half_shard(down_other, 0), half_shard(down_other, 0), 7, up))
    ag_down3.wait_recv()
    ag_down4 = start(remote(half_shard(up_other, 1), half_shard(up_other, 1), 8, down))

    last = len(CHUNKS) - 1
    for p in range(last + 1):
        arrive(p)
        stage_one(p)
        if p:
            stage_three(p - 1)
        stage_two(p)
        if p == 0:
            for copy in (ag_up2, ag_down2, ag_up4, ag_down4):
                copy.wait_recv()
        project(p)
    gate_finish()
    store(gu, ggu_out)
    stage_three(last)

    gg_out[...] = jnp.broadcast_to(jnp.sum(gg_acc[...], axis=1, keepdims=True), gg_out.shape)

    def window(to):
        return gg_out.at[pl.ds(pl.multiple_of(to * SEND - 4 * lax.rem(to, 2), 8), 16)]

    gg_local = small(window, gg_in, 16, 1)
    loads[3].wait()
    loads[4].wait()
    for p in range(last):
        stage_four(p)
    gg_local.wait()
    all_of(gg_in, 16, small_rsem.at[1]).wait()
    row = iota((n_ep * 16, 128), 0) - 4 * lax.rem(e, 2)
    back = gg_in[...]
    for k in range(TOPK):
        for b in range(n_tok // 128):
            cols = slice(b * 128, (b + 1) * 128)
            hit = row == pos16[k : k + 1, cols]
            gate_out[k : k + 1, cols] = jnp.sum(jnp.where(hit, back, 0.0), axis=0, keepdims=True)

    stage_four(last)
    for copy in stores:
        copy.wait()
    for copy in started:
        copy.wait_send()
    all_of(w_out, 16, small_ssem.at[0]).wait()
    all_of(gg_in, 16, small_ssem.at[1]).wait()
    for p in range(len(CHUNKS)):
        all_of(rows_out[p], msg, rows_ssem.at[p]).wait()


def outer(
    n_ep, n_rep,
    ids_ref, slots_ref, gates_ref, og_hbm, gu_hbm, master_hbm, moment1_hbm, moment2_hbm,
    ggu_out, gate_out, master_out, moment1_out, moment2_out, *scratch,
):
    n = len(CHUNKS)
    rows_out, rows_in = scratch[7 : 7 + n], scratch[7 + n : 7 + 2 * n]
    kernel(
        n_ep, n_rep, ids_ref, slots_ref, gates_ref, og_hbm, gu_hbm, master_hbm, moment1_hbm, moment2_hbm,
        ggu_out, gate_out, master_out, moment1_out, moment2_out,
        *scratch[:7], rows_out, rows_in, *scratch[7 + 2 * n :],
    )


def exchange(n_ep, n_rep, ids, slots, gates, out_grad, gate_up, master, moment1, moment2):
    tokens, width = out_grad.shape
    n_slots, two_hidden = gate_up.shape
    n_hidden = two_hidden // 2
    part_rows = master.shape[0]
    pair = 2 * part_rows
    msg = PARTS * SEND
    f32, bf16 = jnp.float32, jnp.bfloat16
    n = len(CHUNKS)
    n_sems = 9 + 7 * n
    vmem = pl.BlockSpec(memory_space=pltpu.VMEM)
    hbm = pl.BlockSpec(memory_space=pl.ANY)
    rows = [pltpu.VMEM((n_ep * msg, size * 128), bf16) for size in CHUNKS]
    dma = pltpu.SemaphoreType.DMA
    return pl.pallas_call(
        functools.partial(outer, n_ep, n_rep),
        out_shape=(
            jax.ShapeDtypeStruct((n_slots, two_hidden), bf16),
            jax.ShapeDtypeStruct((TOPK, tokens), f32),
            jax.ShapeDtypeStruct((part_rows, width), f32),
            jax.ShapeDtypeStruct((part_rows, width), bf16),
            jax.ShapeDtypeStruct((part_rows, width), bf16),
        ),
        in_specs=[vmem, vmem, vmem, hbm, hbm, hbm, hbm, hbm],
        out_specs=(hbm, vmem, hbm, hbm, hbm),
        scratch_shapes=[
            pltpu.VMEM((tokens, width), bf16),
            pltpu.VMEM((n_slots, two_hidden), bf16),
            pltpu.VMEM((part_rows, width), f32),
            pltpu.VMEM((part_rows, width), bf16),
            pltpu.VMEM((part_rows, width), bf16),
            pltpu.VMEM((n_ep * msg, PARTS * tokens), bf16),
            pltpu.VMEM((PARTS * msg, PARTS * msg), bf16),
            *rows,
            *rows,
            pltpu.VMEM((n_ep * 16, 128), bf16),
            pltpu.VMEM((n_ep * 16, 128), bf16),
            pltpu.VMEM((n_slots, width), bf16),
            pltpu.VMEM((n_slots, 128), f32),
            pltpu.VMEM((n_slots, n_hidden), bf16),
            pltpu.VMEM((n_slots, n_hidden), f32),
            pltpu.VMEM((n_slots, n_hidden), f32),
            pltpu.VMEM((n_slots, n_hidden), f32),
            pltpu.VMEM((n_hidden, n_slots), bf16),
            pltpu.VMEM((n_hidden, width), bf16),
            pltpu.VMEM((pair, width), bf16),
            pltpu.VMEM((pair, width), bf16),
            pltpu.VMEM((pair, width), f32),
            pltpu.VMEM((pair, width), bf16),
            pltpu.VMEM((pair, width), bf16),
            pltpu.VMEM((pair, width), bf16),
            pltpu.VMEM((pair, width), bf16),
            pltpu.VMEM((pair, width), f32),
            pltpu.VMEM((part_rows, width), bf16),
            pltpu.VMEM((part_rows, width), bf16),
            pltpu.VMEM((n_slots, 128), f32),
            pltpu.VMEM((n_slots, 128), f32),
            pltpu.VMEM((n_ep * 16, 128), f32),
            dma((5,)),
            dma((1 + 3 * n,)),
            dma((n,)),
            dma((n,)),
            dma((2,)),
            dma((2,)),
            dma((2 + n,)),
            dma((n_sems,)),
            dma((n_sems,)),
        ],
        compiler_params=pltpu.CompilerParams(
            collective_id=0, has_side_effects=True, vmem_limit_bytes=60 * 1024 * 1024
        ),
        name="exchange",
    )(ids, slots, gates, out_grad, gate_up, master, moment1, moment2)


def hand_over(n, *refs):
    given, taken, held = refs[:n], refs[n : 2 * n], refs[2 * n : 3 * n]
    get_sem, put_sem = refs[3 * n :]
    gets = [pltpu.make_async_copy(given[i], held[i], get_sem.at[i]) for i in range(n)]
    puts = [pltpu.make_async_copy(held[i], taken[i], put_sem.at[i]) for i in range(n)]
    for get in gets:
        get.start()
    for get, put in zip(gets, puts):
        get.wait()
        put.start()
    for put in puts:
        put.wait()


def results(*arrays):
    n = len(arrays)
    hbm = pl.BlockSpec(memory_space=pl.ANY)
    sems = pltpu.SemaphoreType.DMA((n,))
    return pl.pallas_call(
        functools.partial(hand_over, n),
        out_shape=tuple(jax.ShapeDtypeStruct(a.shape, a.dtype) for a in arrays),
        in_specs=[hbm] * n,
        out_specs=(hbm,) * n,
        scratch_shapes=[*(pltpu.VMEM(a.shape, a.dtype) for a in arrays), sems, sems],
        compiler_params=pltpu.CompilerParams(vmem_limit_bytes=62 * 1024 * 1024),
        name="results",
    )(*arrays)


def solution(mesh):
    n_ep, n_rep = mesh.shape["ep"], mesh.shape["rep"]

    def per_device(out_grad, expert_ids, slots, gate_weights, saved_gate_up, master, moment1, moment2):
        grad_gate_up, gate_grad, *state = results(
            *exchange(
                n_ep, n_rep, expert_ids.T, slots.T, gate_weights.T,
                out_grad, saved_gate_up[0, 0], master[0], moment1[0], moment2[0],
            )
        )
        return (grad_gate_up.reshape(saved_gate_up.shape), gate_grad.T, *(part[None] for part in state))

    in_specs = (
        P(("rep", "ep"), None),
        P(("rep", "ep"), None),
        P(("rep", "ep"), None),
        P(("rep", "ep"), None),
        P("rep", "ep", None, None),
        P("ep", "rep", None),
        P("ep", "rep", None),
        P("ep", "rep", None),
    )
    out_specs = (
        P("rep", "ep", None, None),
        P(("rep", "ep"), None),
        P("ep", "rep", None),
        P("ep", "rep", None),
        P("ep", "rep", None),
    )
    return jax.shard_map(per_device, mesh=mesh, in_specs=in_specs, out_specs=out_specs, check_vma=False)
```

```python
import functools

import jax
import jax.numpy as jnp
from jax import lax
from jax.experimental import pallas as pl
from jax.experimental.pallas import tpu as pltpu
from jax.sharding import PartitionSpec as P

TOPK = 8
EXP_LOCAL = 8
SEND = 12
PARTS = 4
CHUNKS = (2, 2, 1, 1, 1)
TILE = 512
MESH = pl.DeviceIdType.MESH

beta_one = 0.9
beta_two = 0.95
learn_rate = 0.002
decay_rate = 0.1
adam_eps = 1e-08
adam_step = 50


def adamw(master, moment1, moment2, grad):
    m_new = beta_one * moment1.astype(jnp.float32) + (1.0 - beta_one) * grad
    v_new = beta_two * moment2.astype(jnp.float32) + (1.0 - beta_two) * grad * grad
    corr_one = 1.0 - beta_one**adam_step
    corr_two = 1.0 - beta_two**adam_step
    update = m_new / corr_one / (jnp.sqrt(v_new / corr_two) + adam_eps)
    master_new = master - learn_rate * (update + decay_rate * master)
    return (master_new, m_new.astype(jnp.bfloat16), v_new.astype(jnp.bfloat16))


def iota(shape, dim):
    return lax.broadcasted_iota(jnp.int32, shape, dim)


def div(x, by, top):
    shift = 20
    factor = (1 << shift) // by + 1
    assert all((v * factor) >> shift == v // by for v in range(top)) and top * factor < 2**31
    return (x * factor) >> shift


def kernel(
    n_ep, n_rep,
    ids_ref, slots_ref, gates_ref, og_hbm, gu_hbm, master_hbm, moment1_hbm, moment2_hbm,
    ggu_out, gate_out, master_out, moment1_out, moment2_out,
    og, gu, master, moment1, moment2, pick, unpick,
    rows_out, rows_in, w_out, w_in, dout, wcol,
    hidden, d_silu, silu, proj, scaled_t, shards,
    s1, r1, keep, s2own, r2own, s2sum, r2sum, own, zs, zr,
    gg_acc, gg_out, gg_in,
    load_sem, store_sem, rows_ssem, rows_rsem, small_ssem, small_rsem, local_sem, ssem, rsem,
):
    f32, bf16 = jnp.float32, jnp.bfloat16
    r, e = lax.axis_index("rep"), lax.axis_index("ep")
    y, h = lax.div(r, 2), lax.rem(r, 2)
    n_y = n_rep // 2
    up = (lax.rem(r + 2, n_rep), e)
    down = (lax.rem(r + n_rep - 2, n_rep), e)
    across = (r + 1 - 2 * h, e)
    width = og.shape[1]
    part_rows = shards.shape[0] // n_rep
    pair = 2 * part_rows
    msg = PARTS * SEND
    offsets = [sum(CHUNKS[:i]) * PARTS * 128 for i in range(len(CHUNKS))]

    def peer(k):
        return lax.rem(e + k, n_ep)

    loads = [
        pltpu.make_async_copy(src, dst, load_sem.at[i])
        for i, (src, dst) in enumerate(
            (
                (og_hbm, og), (master_hbm, master), (gu_hbm, gu),
                (moment1_hbm, moment1), (moment2_hbm, moment2),
            )
        )
    ]
    loads[1].start()

    barrier = pltpu.get_barrier_semaphore()

    def greet(k, _):
        pl.semaphore_signal(barrier, inc=1, device_id=(r, peer(k)), device_id_type=MESH)
        return _

    lax.fori_loop(1, n_ep, greet, 0)
    for other in (up, down, across):
        pl.semaphore_signal(barrier, inc=1, device_id=other, device_id_type=MESH)

    mine = pl.ds(pl.multiple_of(r * part_rows, part_rows), part_rows)
    loads[1].wait()

    def cast(t, _):
        cols = pl.ds(pl.multiple_of(t * TILE, TILE), TILE)
        shards[mine, cols] = master[:, cols].astype(bf16)
        return _

    lax.fori_loop(0, width // TILE, cast, 0)

    def remote(src, dst, i, other):
        return pltpu.make_async_remote_copy(
            src_ref=src, dst_ref=dst, send_sem=ssem.at[i], recv_sem=rsem.at[i],
            device_id=other, device_id_type=MESH,
        )

    for i in (0, 2, 3, 4):
        loads[i].start()
    pl.semaphore_wait(barrier, n_ep - 1 + 3)

    def shard(rep):
        return shards.at[pl.ds(pl.multiple_of(rep * part_rows, part_rows), part_rows)]

    def half_shard(rep, which):
        half = part_rows // 2
        return shards.at[pl.ds(pl.multiple_of(rep * part_rows + which * half, half), half)]

    started = []

    def start(copy):
        copy.start()
        started.append(copy)
        return copy

    ag_up = start(remote(shard(r), shard(r), 0, up))
    ag_down = start(remote(shard(r), shard(r), 1, down))
    ag_z = start(remote(shard(r), shard(r), 4, across))

    ids, slots = ids_ref[...], slots_ref[...]
    live = ((ids & (EXP_LOCAL - 1)) == 0) & (slots >= 0)
    expert = ids >> 3
    pos12 = jnp.where(live, expert * SEND + slots, -64)
    pos16 = jnp.where(live, expert * 16 + slots, -64)
    gates = gates_ref[...].astype(f32)
    n_tok = ids.shape[1]

    def pick_rows(g, _):
        row = iota((PARTS * msg, n_tok), 0)
        dest = div(row, msg, PARTS * msg)
        rest = row - dest * msg
        part = div(rest, SEND, msg)
        target = (dest + g * PARTS) * SEND + rest - part * SEND
        hit = target == pos12[0:1, :]
        for k in range(1, TOPK):
            hit = hit | (target == pos12[k : k + 1, :])
        for q in range(PARTS):
            one = jnp.where(hit & (part == q), 1.0, 0.0).astype(bf16)
            pick[pl.ds(pl.multiple_of(g * PARTS * msg, 16), PARTS * msg), q * n_tok : (q + 1) * n_tok] = one
        return _

    lax.fori_loop(0, n_ep // PARTS, pick_rows, 0)

    def small(src_of, dst, rows, sems):
        def send(k, _):
            to = peer(k)
            pltpu.make_async_remote_copy(
                src_ref=src_of(to), dst_ref=dst.at[pl.ds(pl.multiple_of(e * rows, rows), rows)],
                send_sem=small_ssem.at[sems], recv_sem=small_rsem.at[sems],
                device_id=(r, to), device_id_type=MESH,
            ).start()
            return _

        lax.fori_loop(1, n_ep, send, 0)
        copy = pltpu.make_async_copy(
            src_of(e), dst.at[pl.ds(pl.multiple_of(e * rows, rows), rows)], local_sem.at[sems]
        )
        copy.start()
        return copy

    def all_of(ref, rows, sem):
        part = ref.at[pl.ds(0, (n_ep - 1) * rows)]
        return pltpu.make_async_copy(part, part, sem)

    def weight_rows(b, _):
        row = iota((64, n_tok), 0) + b * 64
        total = jnp.zeros((64, n_tok), f32)
        for k in range(TOPK):
            total += jnp.where(row == pos16[k : k + 1, :], gates[k : k + 1, :], 0.0)
        column = jnp.sum(total, axis=1, keepdims=True)
        w_out[pl.ds(pl.multiple_of(b * 64, 64), 64), :] = jnp.broadcast_to(column, (64, 128)).astype(bf16)
        return _

    lax.fori_loop(0, n_ep * 16 // 64, weight_rows, 0)
    w_local = small(lambda to: w_out.at[pl.ds(pl.multiple_of(to * 16, 16), 16)], w_in, 16, 0)

    loads[0].wait()
    rows_local = []
    for p, size in enumerate(CHUNKS):
        wide = size * 128
        out, into = rows_out[p], rows_in[p]

        def gather(g, _, out=out, wide=wide, p=p):
            where = pl.ds(pl.multiple_of(g * PARTS * msg, 16), PARTS * msg)
            total = jnp.zeros((PARTS * msg, wide), f32)
            for q in range(PARTS):
                total += jnp.dot(
                    pick[where, q * n_tok : (q + 1) * n_tok],
                    og[:, offsets[p] + q * wide : offsets[p] + (q + 1) * wide],
                    preferred_element_type=f32,
                )
            out[where, :] = total.astype(bf16)
            return _

        lax.fori_loop(0, n_ep // PARTS, gather, 0)

        def block(ref, i):
            return ref.at[pl.ds(pl.multiple_of(i * msg, 16), msg)]

        def send(k, _, out=out, into=into, p=p):
            to = peer(k * 5)
            pltpu.make_async_remote_copy(
                src_ref=block(out, to), dst_ref=block(into, e),
                send_sem=rows_ssem.at[p], recv_sem=rows_rsem.at[p],
                device_id=(r, to), device_id_type=MESH,
            ).start()
            return _

        lax.fori_loop(1, n_ep, send, 0)
        copy = pltpu.make_async_copy(block(out, e), block(into, e), local_sem.at[2 + p])
        copy.start()
        rows_local.append(copy)

    loads[2].wait()
    n_hidden = hidden.shape[1]
    step = 128

    def activation(t, _):
        cols = pl.ds(pl.multiple_of(t * step, step), step)
        up_cols = pl.ds(pl.multiple_of(n_hidden + t * step, step), step)
        gate, lift = gu[:, cols].astype(f32), gu[:, up_cols].astype(f32)
        sig = jax.nn.sigmoid(gate)
        act = gate * sig
        hidden[:, cols] = (act * lift).astype(bf16)
        silu[:, cols] = act
        d_silu[:, cols] = lift * sig * (1.0 + gate * (1.0 - sig))
        return _

    lax.fori_loop(0, n_hidden // step, activation, 0)
    side = PARTS * msg
    row = iota((side, side), 0)
    part = div(row, msg, side)
    rest = row - part * msg
    dest = div(rest, SEND, msg)
    unpick[...] = jnp.where(
        iota((side, side), 1) == dest * msg + part * SEND + rest - dest * SEND, 1.0, 0.0
    ).astype(bf16)

    ag_up.wait_recv()
    ag_up2 = start(remote(half_shard(down[0], 0), half_shard(down[0], 0), 2, up))
    ag_down.wait_recv()
    ag_down2 = start(remote(half_shard(up[0], 1), half_shard(up[0], 1), 3, down))

    w_local.wait()
    all_of(w_in, 16, small_rsem.at[0]).wait()
    n_slots = n_ep * SEND
    row = iota((n_slots, n_ep * 16), 0)
    dest = div(row, SEND, n_slots)
    order = jnp.where(iota(row.shape, 1) == row + dest * (16 - SEND), 1.0, 0.0).astype(bf16)
    wcol[...] = jnp.dot(order, w_in[...], preferred_element_type=f32)

    def scale(t, _):
        cols = pl.ds(pl.multiple_of(t * step, step), step)
        value = wcol[...] * hidden[:, cols].astype(f32)
        scaled_t[cols, :] = value.astype(bf16).astype(f32).T.astype(bf16)
        return _

    lax.fori_loop(0, n_hidden // step, scale, 0)

    def span(p):
        return pl.ds(offsets[p], CHUNKS[p] * PARTS * 128)

    def tiles(p, body):
        def one(t, _):
            body(pl.ds(pl.multiple_of(offsets[p] + t * TILE, TILE), TILE))
            return _

        lax.fori_loop(0, CHUNKS[p] * PARTS * 128 // TILE, one, 0)

    def arrive(p):
        wide = CHUNKS[p] * 128
        rows_local[p].wait()
        all_of(rows_in[p], msg, rows_rsem.at[p]).wait()

        def restore(g, _):
            got = jnp.dot(
                unpick[...],
                rows_in[p][pl.ds(pl.multiple_of(g * side, 16), side), :],
                preferred_element_type=f32,
            ).astype(bf16)
            for q in range(PARTS):
                dout[pl.ds(pl.multiple_of(g * msg, 16), msg), offsets[p] + q * wide : offsets[p] + (q + 1) * wide] = (
                    got[q * msg : (q + 1) * msg]
                )
            return _

        lax.fori_loop(0, n_ep // PARTS, restore, 0)

    def product(to_y, cols):
        rows = pl.ds(pl.multiple_of(to_y * pair, pair), pair)
        return jnp.dot(scaled_t[rows, :], dout[:, cols], preferred_element_type=f32)

    y_up, y_down, y_far = lax.rem(y + 1, n_y), lax.rem(y + n_y - 1, n_y), lax.rem(y + 2, n_y)
    first, second = pl.ds(0, part_rows), pl.ds(part_rows, part_rows)
    base = 9
    flights = {}

    def stage_one(p):
        def far(cols):
            s1[:, cols] = product(y_far, cols).astype(bf16)

        tiles(p, far)
        i = base + 7 * p
        flights[p, "a"] = start(remote(s1.at[first, span(p)], r1.at[first, span(p)], i, up))
        flights[p, "b"] = start(remote(s1.at[second, span(p)], r1.at[second, span(p)], i + 1, down))

        def near(cols):
            got = product(y_up, cols)
            keep[first, cols] = got[:part_rows]
            s2own[second, cols] = got[part_rows:].astype(bf16)
            got = product(y_down, cols)
            s2own[first, cols] = got[:part_rows].astype(bf16)
            keep[second, cols] = got[part_rows:]

        tiles(p, near)
        flights[p, "own_b"] = start(remote(s2own.at[second, span(p)], r2own.at[second, span(p)], i + 2, up))
        flights[p, "own_a"] = start(remote(s2own.at[first, span(p)], r2own.at[first, span(p)], i + 3, down))

        def here(cols):
            own[:, cols] = product(y, cols)

        tiles(p, here)

    def stage_two(p):
        i = base + 7 * p
        for name, rows, other, j in (("a", first, up, i + 4), ("b", second, down, i + 5)):
            flights[p, name].wait_recv()

            def add(cols, rows=rows):
                s2sum[rows, cols] = (keep[rows, cols] + r1[rows, cols].astype(f32)).astype(bf16)

            tiles(p, add)
            flights[p, "sum_" + name] = start(remote(s2sum.at[rows, span(p)], r2sum.at[rows, span(p)], j, other))

    def half(which, cols):
        rows = pl.ds(pl.multiple_of(which * part_rows, part_rows), part_rows)
        return own[rows, cols] + (r2own[rows, cols].astype(f32) + r2sum[rows, cols].astype(f32))

    def stage_three(p):
        for name in ("own_a", "own_b", "sum_a", "sum_b"):
            flights[p, name].wait_recv()

        def other(cols):
            zs[:, cols] = half(1 - h, cols).astype(bf16)

        tiles(p, other)
        flights[p, "z"] = start(remote(zs.at[:, span(p)], zr.at[:, span(p)], base + 7 * p + 6, across))

    stores = []

    def store(src, dst):
        copy = pltpu.make_async_copy(src, dst, store_sem.at[len(stores)])
        copy.start()
        stores.append(copy)

    def stage_four(p):
        flights[p, "z"].wait_recv()

        def finish(cols):
            grad = half(h, cols) + zr[:, cols].astype(f32)
            master[:, cols], moment1[:, cols], moment2[:, cols] = adamw(
                master[:, cols], moment1[:, cols], moment2[:, cols], grad
            )

        tiles(p, finish)
        for src, dst in ((master, master_out), (moment1, moment1_out), (moment2, moment2_out)):
            store(src.at[:, span(p)], dst.at[:, span(p)])

    def project(p):
        def block(b, _):
            rows = pl.ds(pl.multiple_of(b * pair, pair), pair)
            got = lax.dot_general(
                dout[:, span(p)], shards[rows, span(p)], (((1,), (1,)), ((), ())), preferred_element_type=f32
            )
            proj[:, rows] = got if p == 0 else proj[:, rows] + got
            return _

        lax.fori_loop(0, n_hidden // pair, block, 0)

    def gate_finish():
        def block(t, _):
            cols = pl.ds(pl.multiple_of(t * step, step), step)
            up_cols = pl.ds(pl.multiple_of(n_hidden + t * step, step), step)
            value = proj[:, cols]
            gg_acc[...] += hidden[:, cols].astype(f32) * value
            grad_hidden = wcol[...] * value
            gu[:, cols] = (grad_hidden * d_silu[:, cols]).astype(bf16)
            gu[:, up_cols] = (grad_hidden * silu[:, cols]).astype(bf16)
            return _

        lax.fori_loop(0, n_hidden // step, block, 0)

    gg_acc[...] = jnp.zeros_like(gg_acc)

    up_other, down_other = lax.rem(across[0] + 2, n_rep), lax.rem(across[0] + n_rep - 2, n_rep)
    ag_z.wait_recv()
    ag_up3 = start(remote(shard(across[0]), shard(across[0]), 5, up))
    ag_down3 = start(remote(shard(across[0]), shard(across[0]), 6, down))
    ag_up3.wait_recv()
    ag_up4 = start(remote(half_shard(down_other, 0), half_shard(down_other, 0), 7, up))
    ag_down3.wait_recv()
    ag_down4 = start(remote(half_shard(up_other, 1), half_shard(up_other, 1), 8, down))

    last = len(CHUNKS) - 1
    for p in range(last + 1):
        arrive(p)
        stage_one(p)
        if p:
            stage_three(p - 1)
        stage_two(p)
        if p == 0:
            for copy in (ag_up2, ag_down2, ag_up4, ag_down4):
                copy.wait_recv()
        project(p)
    gate_finish()
    store(gu, ggu_out)
    stage_three(last)

    gg_out[...] = jnp.broadcast_to(jnp.sum(gg_acc[...], axis=1, keepdims=True), gg_out.shape)

    def window(to):
        return gg_out.at[pl.ds(pl.multiple_of(to * SEND - 4 * lax.rem(to, 2), 8), 16)]

    gg_local = small(window, gg_in, 16, 1)
    loads[3].wait()
    loads[4].wait()
    for p in range(last):
        stage_four(p)
    gg_local.wait()
    all_of(gg_in, 16, small_rsem.at[1]).wait()
    row = iota((n_ep * 16, 128), 0) - 4 * lax.rem(e, 2)
    back = gg_in[...]
    for k in range(TOPK):
        for b in range(n_tok // 128):
            cols = slice(b * 128, (b + 1) * 128)
            hit = row == pos16[k : k + 1, cols]
            gate_out[k : k + 1, cols] = jnp.sum(jnp.where(hit, back, 0.0), axis=0, keepdims=True)

    stage_four(last)
    for copy in stores:
        copy.wait()
    for copy in started:
        copy.wait_send()
    all_of(w_out, 16, small_ssem.at[0]).wait()
    all_of(gg_in, 16, small_ssem.at[1]).wait()
    for p in range(len(CHUNKS)):
        all_of(rows_out[p], msg, rows_ssem.at[p]).wait()


def outer(
    n_ep, n_rep,
    ids_ref, slots_ref, gates_ref, og_hbm, gu_hbm, master_hbm, moment1_hbm, moment2_hbm,
    ggu_out, gate_out, master_out, moment1_out, moment2_out, *scratch,
):
    n = len(CHUNKS)
    rows_out, rows_in = scratch[7 : 7 + n], scratch[7 + n : 7 + 2 * n]
    kernel(
        n_ep, n_rep, ids_ref, slots_ref, gates_ref, og_hbm, gu_hbm, master_hbm, moment1_hbm, moment2_hbm,
        ggu_out, gate_out, master_out, moment1_out, moment2_out,
        *scratch[:7], rows_out, rows_in, *scratch[7 + 2 * n :],
    )


def exchange(n_ep, n_rep, ids, slots, gates, out_grad, gate_up, master, moment1, moment2):
    tokens, width = out_grad.shape
    n_slots, two_hidden = gate_up.shape
    n_hidden = two_hidden // 2
    part_rows = master.shape[0]
    pair = 2 * part_rows
    msg = PARTS * SEND
    f32, bf16 = jnp.float32, jnp.bfloat16
    n = len(CHUNKS)
    n_sems = 9 + 7 * n
    vmem = pl.BlockSpec(memory_space=pltpu.VMEM)
    hbm = pl.BlockSpec(memory_space=pl.ANY)
    rows = [pltpu.VMEM((n_ep * msg, size * 128), bf16) for size in CHUNKS]
    dma = pltpu.SemaphoreType.DMA
    return pl.pallas_call(
        functools.partial(outer, n_ep, n_rep),
        out_shape=(
            jax.ShapeDtypeStruct((n_slots, two_hidden), bf16),
            jax.ShapeDtypeStruct((TOPK, tokens), f32),
            jax.ShapeDtypeStruct((part_rows, width), f32),
            jax.ShapeDtypeStruct((part_rows, width), bf16),
            jax.ShapeDtypeStruct((part_rows, width), bf16),
        ),
        in_specs=[vmem, vmem, vmem, hbm, hbm, hbm, hbm, hbm],
        out_specs=(hbm, vmem, hbm, hbm, hbm),
        scratch_shapes=[
            pltpu.VMEM((tokens, width), bf16),
            pltpu.VMEM((n_slots, two_hidden), bf16),
            pltpu.VMEM((part_rows, width), f32),
            pltpu.VMEM((part_rows, width), bf16),
            pltpu.VMEM((part_rows, width), bf16),
            pltpu.VMEM((n_ep * msg, PARTS * tokens), bf16),
            pltpu.VMEM((PARTS * msg, PARTS * msg), bf16),
            *rows,
            *rows,
            pltpu.VMEM((n_ep * 16, 128), bf16),
            pltpu.VMEM((n_ep * 16, 128), bf16),
            pltpu.VMEM((n_slots, width), bf16),
            pltpu.VMEM((n_slots, 128), f32),
            pltpu.VMEM((n_slots, n_hidden), bf16),
            pltpu.VMEM((n_slots, n_hidden), f32),
            pltpu.VMEM((n_slots, n_hidden), f32),
            pltpu.VMEM((n_slots, n_hidden), f32),
            pltpu.VMEM((n_hidden, n_slots), bf16),
            pltpu.VMEM((n_hidden, width), bf16),
            pltpu.VMEM((pair, width), bf16),
            pltpu.VMEM((pair, width), bf16),
            pltpu.VMEM((pair, width), f32),
            pltpu.VMEM((pair, width), bf16),
            pltpu.VMEM((pair, width), bf16),
            pltpu.VMEM((pair, width), bf16),
            pltpu.VMEM((pair, width), bf16),
            pltpu.VMEM((pair, width), f32),
            pltpu.VMEM((part_rows, width), bf16),
            pltpu.VMEM((part_rows, width), bf16),
            pltpu.VMEM((n_slots, 128), f32),
            pltpu.VMEM((n_slots, 128), f32),
            pltpu.VMEM((n_ep * 16, 128), f32),
            dma((5,)),
            dma((1 + 3 * n,)),
            dma((n,)),
            dma((n,)),
            dma((2,)),
            dma((2,)),
            dma((2 + n,)),
            dma((n_sems,)),
            dma((n_sems,)),
        ],
        compiler_params=pltpu.CompilerParams(
            collective_id=0, has_side_effects=True, vmem_limit_bytes=60 * 1024 * 1024
        ),
        name="exchange",
    )(ids, slots, gates, out_grad, gate_up, master, moment1, moment2)


def hand_over(n, *refs):
    given, taken, held = refs[:n], refs[n : 2 * n], refs[2 * n : 3 * n]
    get_sem, put_sem = refs[3 * n :]
    largest_first = sorted(range(n), key=lambda i: -given[i].size * given[i].dtype.itemsize)
    gets = [pltpu.make_async_copy(given[i], held[i], get_sem.at[i]) for i in largest_first]
    puts = [pltpu.make_async_copy(held[i], taken[i], put_sem.at[i]) for i in largest_first]
    for get in gets:
        get.start()
    for get, put in zip(gets, puts):
        get.wait()
        put.start()
    for put in puts:
        put.wait()


def results(*arrays):
    n = len(arrays)
    hbm = pl.BlockSpec(memory_space=pl.ANY)
    sems = pltpu.SemaphoreType.DMA((n,))
    return pl.pallas_call(
        functools.partial(hand_over, n),
        out_shape=tuple(jax.ShapeDtypeStruct(a.shape, a.dtype) for a in arrays),
        in_specs=[hbm] * n,
        out_specs=(hbm,) * n,
        scratch_shapes=[*(pltpu.VMEM(a.shape, a.dtype) for a in arrays), sems, sems],
        compiler_params=pltpu.CompilerParams(vmem_limit_bytes=62 * 1024 * 1024),
        name="results",
    )(*arrays)


def solution(mesh):
    n_ep, n_rep = mesh.shape["ep"], mesh.shape["rep"]

    def per_device(out_grad, expert_ids, slots, gate_weights, saved_gate_up, master, moment1, moment2):
        grad_gate_up, gate_grad, *state = results(
            *exchange(
                n_ep, n_rep, expert_ids.T, slots.T, gate_weights.T,
                out_grad, saved_gate_up[0, 0], master[0], moment1[0], moment2[0],
            )
        )
        return (grad_gate_up.reshape(saved_gate_up.shape), gate_grad.T, *(part[None] for part in state))

    in_specs = (
        P(("rep", "ep"), None),
        P(("rep", "ep"), None),
        P(("rep", "ep"), None),
        P(("rep", "ep"), None),
        P("rep", "ep", None, None),
        P("ep", "rep", None),
        P("ep", "rep", None),
        P("ep", "rep", None),
    )
    out_specs = (
        P("rep", "ep", None, None),
        P(("rep", "ep"), None),
        P("ep", "rep", None),
        P("ep", "rep", None),
        P("ep", "rep", None),
    )
    return jax.shard_map(per_device, mesh=mesh, in_specs=in_specs, out_specs=out_specs, check_vma=False)
```

```python
import functools

import jax
import jax.numpy as jnp
from jax import lax
from jax.experimental import pallas as pl
from jax.experimental.pallas import tpu as pltpu
from jax.sharding import PartitionSpec as P

TOPK = 8
EXP_LOCAL = 8
SEND = 12
PARTS = 4
CHUNKS = (2, 2, 1, 1, 1)
TILE = 512
MESH = pl.DeviceIdType.MESH

beta_one = 0.9
beta_two = 0.95
learn_rate = 0.002
decay_rate = 0.1
adam_eps = 1e-08
adam_step = 50


def adamw(master, moment1, moment2, grad):
    m_new = beta_one * moment1.astype(jnp.float32) + (1.0 - beta_one) * grad
    v_new = beta_two * moment2.astype(jnp.float32) + (1.0 - beta_two) * grad * grad
    corr_one = 1.0 - beta_one**adam_step
    corr_two = 1.0 - beta_two**adam_step
    update = m_new / corr_one / (jnp.sqrt(v_new / corr_two) + adam_eps)
    master_new = master - learn_rate * (update + decay_rate * master)
    return (master_new, m_new.astype(jnp.bfloat16), v_new.astype(jnp.bfloat16))


def iota(shape, dim):
    return lax.broadcasted_iota(jnp.int32, shape, dim)


def div(x, by, top):
    shift = 20
    factor = (1 << shift) // by + 1
    assert all((v * factor) >> shift == v // by for v in range(top)) and top * factor < 2**31
    return (x * factor) >> shift


def kernel(
    n_ep, n_rep,
    ids_ref, slots_ref, gates_ref, og_hbm, gu_hbm, master_hbm, moment1_hbm, moment2_hbm,
    ggu_out, gate_out, master_out, moment1_out, moment2_out,
    og, gu, master, moment1, moment2, pick, unpick,
    rows_out, rows_in, w_out, w_in, dout, wcol,
    hidden, d_silu, silu, proj, scaled_t, shards,
    s1, r1, keep, s2own, r2own, s2sum, r2sum, own, zs, zr,
    gg_acc, gg_out, gg_in,
    load_sem, store_sem, rows_ssem, rows_rsem, small_ssem, small_rsem, local_sem, ssem, rsem,
):
    f32, bf16 = jnp.float32, jnp.bfloat16
    r, e = lax.axis_index("rep"), lax.axis_index("ep")
    y, h = lax.div(r, 2), lax.rem(r, 2)
    n_y = n_rep // 2
    up = (lax.rem(r + 2, n_rep), e)
    down = (lax.rem(r + n_rep - 2, n_rep), e)
    across = (r + 1 - 2 * h, e)
    width = og.shape[1]
    part_rows = shards.shape[0] // n_rep
    pair = 2 * part_rows
    msg = PARTS * SEND
    offsets = [sum(CHUNKS[:i]) * PARTS * 128 for i in range(len(CHUNKS))]

    def peer(k):
        return lax.rem(e + k, n_ep)

    loads = [
        pltpu.make_async_copy(src, dst, load_sem.at[i])
        for i, (src, dst) in enumerate(
            (
                (og_hbm, og), (master_hbm, master), (gu_hbm, gu),
                (moment1_hbm, moment1), (moment2_hbm, moment2),
            )
        )
    ]
    loads[1].start()

    barrier = pltpu.get_barrier_semaphore()

    def greet(k, _):
        pl.semaphore_signal(barrier, inc=1, device_id=(r, peer(k)), device_id_type=MESH)
        return _

    lax.fori_loop(1, n_ep, greet, 0)
    for other in (up, down, across):
        pl.semaphore_signal(barrier, inc=1, device_id=other, device_id_type=MESH)

    mine = pl.ds(pl.multiple_of(r * part_rows, part_rows), part_rows)
    loads[1].wait()

    def cast(t, _):
        cols = pl.ds(pl.multiple_of(t * TILE, TILE), TILE)
        shards[mine, cols] = master[:, cols].astype(bf16)
        return _

    lax.fori_loop(0, width // TILE, cast, 0)

    def remote(src, dst, i, other):
        return pltpu.make_async_remote_copy(
            src_ref=src, dst_ref=dst, send_sem=ssem.at[i], recv_sem=rsem.at[i],
            device_id=other, device_id_type=MESH,
        )

    for i in (0, 2, 3, 4):
        loads[i].start()
    pl.semaphore_wait(barrier, n_ep - 1 + 3)

    def shard(rep):
        return shards.at[pl.ds(pl.multiple_of(rep * part_rows, part_rows), part_rows)]

    def half_shard(rep, which):
        half = part_rows // 2
        return shards.at[pl.ds(pl.multiple_of(rep * part_rows + which * half, half), half)]

    started = []

    def start(copy):
        copy.start()
        started.append(copy)
        return copy

    ag_z = start(remote(shard(r), shard(r), 4, across))
    ag_up = start(remote(shard(r), shard(r), 0, up))
    ag_down = start(remote(shard(r), shard(r), 1, down))

    ids, slots = ids_ref[...], slots_ref[...]
    live = ((ids & (EXP_LOCAL - 1)) == 0) & (slots >= 0)
    expert = ids >> 3
    pos12 = jnp.where(live, expert * SEND + slots, -64)
    pos16 = jnp.where(live, expert * 16 + slots, -64)
    gates = gates_ref[...].astype(f32)
    n_tok = ids.shape[1]

    def pick_rows(g, _):
        row = iota((PARTS * msg, n_tok), 0)
        dest = div(row, msg, PARTS * msg)
        rest = row - dest * msg
        part = div(rest, SEND, msg)
        target = (dest + g * PARTS) * SEND + rest - part * SEND
        hit = target == pos12[0:1, :]
        for k in range(1, TOPK):
            hit = hit | (target == pos12[k : k + 1, :])
        for q in range(PARTS):
            one = jnp.where(hit & (part == q), 1.0, 0.0).astype(bf16)
            pick[pl.ds(pl.multiple_of(g * PARTS * msg, 16), PARTS * msg), q * n_tok : (q + 1) * n_tok] = one
        return _

    lax.fori_loop(0, n_ep // PARTS, pick_rows, 0)

    def small(src_of, dst, rows, sems):
        def send(k, _):
            to = peer(k)
            pltpu.make_async_remote_copy(
                src_ref=src_of(to), dst_ref=dst.at[pl.ds(pl.multiple_of(e * rows, rows), rows)],
                send_sem=small_ssem.at[sems], recv_sem=small_rsem.at[sems],
                device_id=(r, to), device_id_type=MESH,
            ).start()
            return _

        lax.fori_loop(1, n_ep, send, 0)
        copy = pltpu.make_async_copy(
            src_of(e), dst.at[pl.ds(pl.multiple_of(e * rows, rows), rows)], local_sem.at[sems]
        )
        copy.start()
        return copy

    def all_of(ref, rows, sem):
        part = ref.at[pl.ds(0, (n_ep - 1) * rows)]
        return pltpu.make_async_copy(part, part, sem)

    def weight_rows(b, _):
        row = iota((64, n_tok), 0) + b * 64
        total = jnp.zeros((64, n_tok), f32)
        for k in range(TOPK):
            total += jnp.where(row == pos16[k : k + 1, :], gates[k : k + 1, :], 0.0)
        column = jnp.sum(total, axis=1, keepdims=True)
        w_out[pl.ds(pl.multiple_of(b * 64, 64), 64), :] = jnp.broadcast_to(column, (64, 128)).astype(bf16)
        return _

    lax.fori_loop(0, n_ep * 16 // 64, weight_rows, 0)
    w_local = small(lambda to: w_out.at[pl.ds(pl.multiple_of(to * 16, 16), 16)], w_in, 16, 0)

    loads[0].wait()
    rows_local = []
    for p, size in enumerate(CHUNKS):
        wide = size * 128
        out, into = rows_out[p], rows_in[p]

        def gather(g, _, out=out, wide=wide, p=p):
            where = pl.ds(pl.multiple_of(g * PARTS * msg, 16), PARTS * msg)
            total = jnp.zeros((PARTS * msg, wide), f32)
            for q in range(PARTS):
                total += jnp.dot(
                    pick[where, q * n_tok : (q + 1) * n_tok],
                    og[:, offsets[p] + q * wide : offsets[p] + (q + 1) * wide],
                    preferred_element_type=f32,
                )
            out[where, :] = total.astype(bf16)
            return _

        lax.fori_loop(0, n_ep // PARTS, gather, 0)

        def block(ref, i):
            return ref.at[pl.ds(pl.multiple_of(i * msg, 16), msg)]

        def send(k, _, out=out, into=into, p=p):
            to = peer(k)
            pltpu.make_async_remote_copy(
                src_ref=block(out, to), dst_ref=block(into, e),
                send_sem=rows_ssem.at[p], recv_sem=rows_rsem.at[p],
                device_id=(r, to), device_id_type=MESH,
            ).start()
            return _

        lax.fori_loop(1, n_ep, send, 0)
        copy = pltpu.make_async_copy(block(out, e), block(into, e), local_sem.at[2 + p])
        copy.start()
        rows_local.append(copy)

    loads[2].wait()
    n_hidden = hidden.shape[1]
    step = 128

    def activation(t, _):
        cols = pl.ds(pl.multiple_of(t * step, step), step)
        up_cols = pl.ds(pl.multiple_of(n_hidden + t * step, step), step)
        gate, lift = gu[:, cols].astype(f32), gu[:, up_cols].astype(f32)
        sig = jax.nn.sigmoid(gate)
        act = gate * sig
        hidden[:, cols] = (act * lift).astype(bf16)
        silu[:, cols] = act
        d_silu[:, cols] = lift * sig * (1.0 + gate * (1.0 - sig))
        return _

    lax.fori_loop(0, n_hidden // step, activation, 0)
    side = PARTS * msg
    row = iota((side, side), 0)
    part = div(row, msg, side)
    rest = row - part * msg
    dest = div(rest, SEND, msg)
    unpick[...] = jnp.where(
        iota((side, side), 1) == dest * msg + part * SEND + rest - dest * SEND, 1.0, 0.0
    ).astype(bf16)

    ag_up.wait_recv()
    ag_up2 = start(remote(half_shard(down[0], 0), half_shard(down[0], 0), 2, up))
    ag_down.wait_recv()
    ag_down2 = start(remote(half_shard(up[0], 1), half_shard(up[0], 1), 3, down))

    w_local.wait()
    all_of(w_in, 16, small_rsem.at[0]).wait()
    n_slots = n_ep * SEND
    row = iota((n_slots, n_ep * 16), 0)
    dest = div(row, SEND, n_slots)
    order = jnp.where(iota(row.shape, 1) == row + dest * (16 - SEND), 1.0, 0.0).astype(bf16)
    wcol[...] = jnp.dot(order, w_in[...], preferred_element_type=f32)

    def scale(t, _):
        cols = pl.ds(pl.multiple_of(t * step, step), step)
        value = wcol[...] * hidden[:, cols].astype(f32)
        scaled_t[cols, :] = value.astype(bf16).astype(f32).T.astype(bf16)
        return _

    lax.fori_loop(0, n_hidden // step, scale, 0)

    def span(p):
        return pl.ds(offsets[p], CHUNKS[p] * PARTS * 128)

    def tiles(p, body):
        def one(t, _):
            body(pl.ds(pl.multiple_of(offsets[p] + t * TILE, TILE), TILE))
            return _

        lax.fori_loop(0, CHUNKS[p] * PARTS * 128 // TILE, one, 0)

    def arrive(p):
        wide = CHUNKS[p] * 128
        rows_local[p].wait()
        all_of(rows_in[p], msg, rows_rsem.at[p]).wait()

        def restore(g, _):
            got = jnp.dot(
                unpick[...],
                rows_in[p][pl.ds(pl.multiple_of(g * side, 16), side), :],
                preferred_element_type=f32,
            ).astype(bf16)
            for q in range(PARTS):
                dout[pl.ds(pl.multiple_of(g * msg, 16), msg), offsets[p] + q * wide : offsets[p] + (q + 1) * wide] = (
                    got[q * msg : (q + 1) * msg]
                )
            return _

        lax.fori_loop(0, n_ep // PARTS, restore, 0)

    def product(to_y, cols):
        rows = pl.ds(pl.multiple_of(to_y * pair, pair), pair)
        return jnp.dot(scaled_t[rows, :], dout[:, cols], preferred_element_type=f32)

    y_up, y_down, y_far = lax.rem(y + 1, n_y), lax.rem(y + n_y - 1, n_y), lax.rem(y + 2, n_y)
    first, second = pl.ds(0, part_rows), pl.ds(part_rows, part_rows)
    base = 9
    flights = {}

    def stage_one(p):
        def far(cols):
            s1[:, cols] = product(y_far, cols).astype(bf16)

        tiles(p, far)
        i = base + 7 * p
        flights[p, "a"] = start(remote(s1.at[first, span(p)], r1.at[first, span(p)], i, up))
        flights[p, "b"] = start(remote(s1.at[second, span(p)], r1.at[second, span(p)], i + 1, down))

        def near(cols):
            got = product(y_up, cols)
            keep[first, cols] = got[:part_rows]
            s2own[second, cols] = got[part_rows:].astype(bf16)
            got = product(y_down, cols)
            s2own[first, cols] = got[:part_rows].astype(bf16)
            keep[second, cols] = got[part_rows:]

        tiles(p, near)
        flights[p, "own_b"] = start(remote(s2own.at[second, span(p)], r2own.at[second, span(p)], i + 2, up))
        flights[p, "own_a"] = start(remote(s2own.at[first, span(p)], r2own.at[first, span(p)], i + 3, down))

        def here(cols):
            own[:, cols] = product(y, cols)

        tiles(p, here)

    def stage_two(p):
        i = base + 7 * p
        for name, rows, other, j in (("a", first, up, i + 4), ("b", second, down, i + 5)):
            flights[p, name].wait_recv()

            def add(cols, rows=rows):
                s2sum[rows, cols] = (keep[rows, cols] + r1[rows, cols].astype(f32)).astype(bf16)

            tiles(p, add)
            flights[p, "sum_" + name] = start(remote(s2sum.at[rows, span(p)], r2sum.at[rows, span(p)], j, other))

    def half(which, cols):
        rows = pl.ds(pl.multiple_of(which * part_rows, part_rows), part_rows)
        return own[rows, cols] + (r2own[rows, cols].astype(f32) + r2sum[rows, cols].astype(f32))

    def stage_three(p):
        for name in ("own_a", "own_b", "sum_a", "sum_b"):
            flights[p, name].wait_recv()

        def other(cols):
            zs[:, cols] = half(1 - h, cols).astype(bf16)

        tiles(p, other)
        flights[p, "z"] = start(remote(zs.at[:, span(p)], zr.at[:, span(p)], base + 7 * p + 6, across))

    stores = []

    def store(src, dst):
        copy = pltpu.make_async_copy(src, dst, store_sem.at[len(stores)])
        copy.start()
        stores.append(copy)

    def stage_four(p):
        flights[p, "z"].wait_recv()

        def finish(cols):
            grad = half(h, cols) + zr[:, cols].astype(f32)
            master[:, cols], moment1[:, cols], moment2[:, cols] = adamw(
                master[:, cols], moment1[:, cols], moment2[:, cols], grad
            )

        tiles(p, finish)
        for src, dst in ((master, master_out), (moment1, moment1_out), (moment2, moment2_out)):
            store(src.at[:, span(p)], dst.at[:, span(p)])

    def project(p):
        def block(b, _):
            rows = pl.ds(pl.multiple_of(b * pair, pair), pair)
            got = lax.dot_general(
                dout[:, span(p)], shards[rows, span(p)], (((1,), (1,)), ((), ())), preferred_element_type=f32
            )
            proj[:, rows] = got if p == 0 else proj[:, rows] + got
            return _

        lax.fori_loop(0, n_hidden // pair, block, 0)

    def gate_finish():
        def block(t, _):
            cols = pl.ds(pl.multiple_of(t * step, step), step)
            up_cols = pl.ds(pl.multiple_of(n_hidden + t * step, step), step)
            value = proj[:, cols]
            gg_acc[...] += hidden[:, cols].astype(f32) * value
            grad_hidden = wcol[...] * value
            gu[:, cols] = (grad_hidden * d_silu[:, cols]).astype(bf16)
            gu[:, up_cols] = (grad_hidden * silu[:, cols]).astype(bf16)
            return _

        lax.fori_loop(0, n_hidden // step, block, 0)

    gg_acc[...] = jnp.zeros_like(gg_acc)

    up_other, down_other = lax.rem(across[0] + 2, n_rep), lax.rem(across[0] + n_rep - 2, n_rep)
    ag_z.wait_recv()
    ag_up3 = start(remote(shard(across[0]), shard(across[0]), 5, up))
    ag_down3 = start(remote(shard(across[0]), shard(across[0]), 6, down))
    ag_up3.wait_recv()
    ag_up4 = start(remote(half_shard(down_other, 0), half_shard(down_other, 0), 7, up))
    ag_down3.wait_recv()
    ag_down4 = start(remote(half_shard(up_other, 1), half_shard(up_other, 1), 8, down))

    last = len(CHUNKS) - 1
    for p in range(last + 1):
        arrive(p)
        stage_one(p)
        if p:
            stage_three(p - 1)
        stage_two(p)
        if p == 0:
            for copy in (ag_up2, ag_down2, ag_up4, ag_down4):
                copy.wait_recv()
        if p:
            project(p - 1)
    project(last)
    gate_finish()
    store(gu, ggu_out)
    stage_three(last)

    gg_out[...] = jnp.broadcast_to(jnp.sum(gg_acc[...], axis=1, keepdims=True), gg_out.shape)

    def window(to):
        return gg_out.at[pl.ds(pl.multiple_of(to * SEND - 4 * lax.rem(to, 2), 8), 16)]

    gg_local = small(window, gg_in, 16, 1)
    loads[3].wait()
    loads[4].wait()
    for p in range(last):
        stage_four(p)
    gg_local.wait()
    all_of(gg_in, 16, small_rsem.at[1]).wait()
    row = iota((n_ep * 16, 128), 0) - 4 * lax.rem(e, 2)
    back = gg_in[...]
    for k in range(TOPK):
        for b in range(n_tok // 128):
            cols = slice(b * 128, (b + 1) * 128)
            hit = row == pos16[k : k + 1, cols]
            gate_out[k : k + 1, cols] = jnp.sum(jnp.where(hit, back, 0.0), axis=0, keepdims=True)

    stage_four(last)
    for copy in stores:
        copy.wait()
    for copy in started:
        copy.wait_send()
    all_of(w_out, 16, small_ssem.at[0]).wait()
    all_of(gg_in, 16, small_ssem.at[1]).wait()
    for p in range(len(CHUNKS)):
        all_of(rows_out[p], msg, rows_ssem.at[p]).wait()


def outer(
    n_ep, n_rep,
    ids_ref, slots_ref, gates_ref, og_hbm, gu_hbm, master_hbm, moment1_hbm, moment2_hbm,
    ggu_out, gate_out, master_out, moment1_out, moment2_out, *scratch,
):
    n = len(CHUNKS)
    rows_out, rows_in = scratch[7 : 7 + n], scratch[7 + n : 7 + 2 * n]
    kernel(
        n_ep, n_rep, ids_ref, slots_ref, gates_ref, og_hbm, gu_hbm, master_hbm, moment1_hbm, moment2_hbm,
        ggu_out, gate_out, master_out, moment1_out, moment2_out,
        *scratch[:7], rows_out, rows_in, *scratch[7 + 2 * n :],
    )


def exchange(n_ep, n_rep, ids, slots, gates, out_grad, gate_up, master, moment1, moment2):
    tokens, width = out_grad.shape
    n_slots, two_hidden = gate_up.shape
    n_hidden = two_hidden // 2
    part_rows = master.shape[0]
    pair = 2 * part_rows
    msg = PARTS * SEND
    f32, bf16 = jnp.float32, jnp.bfloat16
    n = len(CHUNKS)
    n_sems = 9 + 7 * n
    vmem = pl.BlockSpec(memory_space=pltpu.VMEM)
    hbm = pl.BlockSpec(memory_space=pl.ANY)
    rows = [pltpu.VMEM((n_ep * msg, size * 128), bf16) for size in CHUNKS]
    dma = pltpu.SemaphoreType.DMA
    return pl.pallas_call(
        functools.partial(outer, n_ep, n_rep),
        out_shape=(
            jax.ShapeDtypeStruct((n_slots, two_hidden), bf16),
            jax.ShapeDtypeStruct((TOPK, tokens), f32),
            jax.ShapeDtypeStruct((part_rows, width), f32),
            jax.ShapeDtypeStruct((part_rows, width), bf16),
            jax.ShapeDtypeStruct((part_rows, width), bf16),
        ),
        in_specs=[vmem, vmem, vmem, hbm, hbm, hbm, hbm, hbm],
        out_specs=(hbm, vmem, hbm, hbm, hbm),
        scratch_shapes=[
            pltpu.VMEM((tokens, width), bf16),
            pltpu.VMEM((n_slots, two_hidden), bf16),
            pltpu.VMEM((part_rows, width), f32),
            pltpu.VMEM((part_rows, width), bf16),
            pltpu.VMEM((part_rows, width), bf16),
            pltpu.VMEM((n_ep * msg, PARTS * tokens), bf16),
            pltpu.VMEM((PARTS * msg, PARTS * msg), bf16),
            *rows,
            *rows,
            pltpu.VMEM((n_ep * 16, 128), bf16),
            pltpu.VMEM((n_ep * 16, 128), bf16),
            pltpu.VMEM((n_slots, width), bf16),
            pltpu.VMEM((n_slots, 128), f32),
            pltpu.VMEM((n_slots, n_hidden), bf16),
            pltpu.VMEM((n_slots, n_hidden), f32),
            pltpu.VMEM((n_slots, n_hidden), f32),
            pltpu.VMEM((n_slots, n_hidden), f32),
            pltpu.VMEM((n_hidden, n_slots), bf16),
            pltpu.VMEM((n_hidden, width), bf16),
            pltpu.VMEM((pair, width), bf16),
            pltpu.VMEM((pair, width), bf16),
            pltpu.VMEM((pair, width), f32),
            pltpu.VMEM((pair, width), bf16),
            pltpu.VMEM((pair, width), bf16),
            pltpu.VMEM((pair, width), bf16),
            pltpu.VMEM((pair, width), bf16),
            pltpu.VMEM((pair, width), f32),
            pltpu.VMEM((part_rows, width), bf16),
            pltpu.VMEM((part_rows, width), bf16),
            pltpu.VMEM((n_slots, 128), f32),
            pltpu.VMEM((n_slots, 128), f32),
            pltpu.VMEM((n_ep * 16, 128), f32),
            dma((5,)),
            dma((1 + 3 * n,)),
            dma((n,)),
            dma((n,)),
            dma((2,)),
            dma((2,)),
            dma((2 + n,)),
            dma((n_sems,)),
            dma((n_sems,)),
        ],
        compiler_params=pltpu.CompilerParams(
            collective_id=0, has_side_effects=True, vmem_limit_bytes=60 * 1024 * 1024
        ),
        name="exchange",
    )(ids, slots, gates, out_grad, gate_up, master, moment1, moment2)


def hand_over(n, *refs):
    given, taken, held = refs[:n], refs[n : 2 * n], refs[2 * n : 3 * n]
    get_sem, put_sem = refs[3 * n :]
    gets = [pltpu.make_async_copy(given[i], held[i], get_sem.at[i]) for i in range(n)]
    puts = [pltpu.make_async_copy(held[i], taken[i], put_sem.at[i]) for i in range(n)]
    for get in gets:
        get.start()
    for get, put in zip(gets, puts):
        get.wait()
        put.start()
    for put in puts:
        put.wait()


def results(*arrays):
    n = len(arrays)
    hbm = pl.BlockSpec(memory_space=pl.ANY)
    sems = pltpu.SemaphoreType.DMA((n,))
    return pl.pallas_call(
        functools.partial(hand_over, n),
        out_shape=tuple(jax.ShapeDtypeStruct(a.shape, a.dtype) for a in arrays),
        in_specs=[hbm] * n,
        out_specs=(hbm,) * n,
        scratch_shapes=[*(pltpu.VMEM(a.shape, a.dtype) for a in arrays), sems, sems],
        compiler_params=pltpu.CompilerParams(vmem_limit_bytes=62 * 1024 * 1024),
        name="results",
    )(*arrays)


def solution(mesh):
    n_ep, n_rep = mesh.shape["ep"], mesh.shape["rep"]

    def per_device(out_grad, expert_ids, slots, gate_weights, saved_gate_up, master, moment1, moment2):
        grad_gate_up, gate_grad, *state = results(
            *exchange(
                n_ep, n_rep, expert_ids.T, slots.T, gate_weights.T,
                out_grad, saved_gate_up[0, 0], master[0], moment1[0], moment2[0],
            )
        )
        return (grad_gate_up.reshape(saved_gate_up.shape), gate_grad.T, *(part[None] for part in state))

    in_specs = (
        P(("rep", "ep"), None),
        P(("rep", "ep"), None),
        P(("rep", "ep"), None),
        P(("rep", "ep"), None),
        P("rep", "ep", None, None),
        P("ep", "rep", None),
        P("ep", "rep", None),
        P("ep", "rep", None),
    )
    out_specs = (
        P("rep", "ep", None, None),
        P(("rep", "ep"), None),
        P("ep", "rep", None),
        P("ep", "rep", None),
        P("ep", "rep", None),
    )
    return jax.shard_map(per_device, mesh=mesh, in_specs=in_specs, out_specs=out_specs, check_vma=False)
```
